32 devices in a mesh: grp: 2 (over x), ka: 16 (over z, y, core).
Axes of the slice: x: 2, y: 2, z: 4, core: 2. Of those that a mesh axis runs over, the one named last changes fastest.
Arguments:
- sources: bfloat16 [1024, 512, 64], P('ka', None, 'grp'), parts along dimension 2, may hold values from -6 to 6
- bessel: bfloat16 [512, 1024, 512], P('ka'), may hold values from -0.25 to 0.25
- multipoles: int32 [512], P('ka'), may hold values from 2 to 5000
- window_low: int32 [64], P('grp'), parts along dimension 0, may hold values from 0 to 127
- window_high: int32 [64], P('grp'), parts along dimension 0, may hold values from 384 to 512
- params: float32 [6, 64], P(None, 'grp'), parts along dimension 1, may hold values from -1 to 1
- weight_in: float32 [512, 6], replicated, may hold values from -2.5 to 2.5
- bias_in: float32 [512], replicated, may hold values from -3 to 3
- weight_mid: float32 [512, 512], replicated, may hold values from -0.25 to 0.25
- bias_mid: float32 [512], replicated, may hold values from -3 to 3
- weight_out: float32 [64, 512], replicated, may hold values from -0.25 to 0.25
- bias_out: float32 [64], replicated, may hold values from -4 to 4
- pca_basis: float32 [512, 64], P('ka'), may hold values from -0.75 to 0.75
- offset: float32 [512], P('ka'), may hold values from -4 to 4
Outputs:
- spectra: float32 [512, 64], P('ka', 'grp'), parts along dimension 1
- grad_basis: float32 [1024, 64], P(('grp', 'ka')), parts along dimension 0
- grad_weight_in: float32 [1024, 6], P('grp'), parts along dimension 0
- grad_weight_mid: float32 [1024, 512], P('grp'), parts along dimension 0
- grad_weight_out: float32 [128, 512], P('grp'), parts along dimension 0
The draws below stay inside these ranges and needn't reach their ends.
There are 2 independent parts, one for each index of `grp`. The reference program is written for one: setup_inputs(seed, part) draws one part's arguments, and reference() takes and returns one part's arrays. A program takes and returns all parts, laid end to end along the dimension named above; an argument that names none is the same for every part. Nothing has to cross between parts.
All inputs are finite; a program needn't handle non-finite values.
Results may differ from the reference program's by a relative error of at most 0.0003.
Values may be sent and summed in bfloat16 or wider, within the bound.
No kernel may reach another device: no remote copies, remote signals or barrier semaphores. Data moves between devices by JAX's collectives and lax.ppermute only.
A program may use at most 128 MiB of HBM per device.

```python
import math
import jax
import jax.numpy as jnp
from jax import lax

NT = 1024
NK = 512
NL = 512
LMAX = 5000
NPAR = 6
HID = 512
PCA = 64
C = 32


def place_ends(array, own_key, smallest, largest):
    extent = array.shape
    index_at = [jax.random.randint(jax.random.fold_in(own_key, axis), (), 0, extent[axis]) for axis in range(len(extent))]
    array = array.at[tuple(index_at)].set(smallest)
    longest = extent.index(max(extent))
    index_at[longest] = (index_at[longest] + 1) % extent[longest]
    return array.at[tuple(index_at)].set(largest)


def raised(result, own_key, source, target, parts, factor):
    def block_of(dim):
        return (jnp.arange(result.shape[dim]) // (result.shape[dim] // parts)).reshape((-1,) + (1,) * (result.ndim - 1 - dim))

    near = jax.random.permutation(own_key, parts)[block_of(target)]
    second = (block_of(target) + parts // 2) % parts
    return jnp.where((block_of(source) == near) | (block_of(source) == second), factor * result, result)


def block_levels(stream_key, dims, pieces, smallest, top_value):
    factor_of, own = 1.0, jax.random.fold_in(stream_key, 6)
    for position, parts in pieces:
        steps = jnp.exp(jax.random.uniform(jax.random.fold_in(own, position), (parts,), jnp.float32, smallest / len(pieces), top_value / len(pieces)))
        factor_of = factor_of * jnp.repeat(steps, dims[position] // parts).reshape([-1 if axis == position else 1 for axis in range(len(dims))])
    return factor_of


def noise(own_key, shape, width, reach, cuts=(), kind=jnp.bfloat16):
    drawn = jax.random.normal(own_key, shape, jnp.float32) * width
    if len(cuts) > 0:
        drawn = block_levels(own_key, shape, cuts, -0.22, 0.18) * drawn
    return jnp.clip(drawn, min=-reach, max=reach).astype(kind)


def bell_draw_with(key, extent, scale, most, split, heavy, kind=jnp.bfloat16):
    drawn = scale * jax.random.normal(key, extent, jnp.float32)
    if split:
        drawn = drawn * block_levels(key, extent, split, -0.22, 0.18)
    return jnp.clip(raised(drawn, jax.random.fold_in(key, 3), *heavy), -most, most).astype(kind)


def setup_inputs(seed: int = 0, part: int = 0) -> dict:
    splits = jax.random.split(jax.random.key(seed), 15)
    part_splits = jax.random.split(jax.random.fold_in(splits[14], part), 15)
    sources = noise(part_splits[0], (NT, NK, C), 1.0, 6.0, ((0, 16),))
    bessel = bell_draw_with(splits[1], (NK, NT, NL), NT ** -0.5, 0.25, ((0, 16),), (0, 2, 16, 2.0))
    multipoles = place_ends(jax.random.randint(splits[2], (NL,), 2, LMAX + 1), jax.random.fold_in(splits[2], 1), 2, LMAX).astype(jnp.int32)
    window_low = place_ends(jax.random.randint(part_splits[3], (C,), 0, NK // 4), jax.random.fold_in(part_splits[3], 1), 0, (NK // 4) - 1).astype(jnp.int32)
    window_high = place_ends(jax.random.randint(part_splits[4], (C,), (3 * NK) // 4, NK + 1), jax.random.fold_in(part_splits[4], 1), (3 * NK) // 4, NK).astype(jnp.int32)
    params = jnp.clip(jax.random.uniform(part_splits[5], (NPAR, C), jnp.float32, -1.0, 1.0), -1.0, 1.0)
    weight_in = noise(splits[6], (HID, NPAR), NPAR ** -0.5, 2.5, (), jnp.float32)
    bias_in = noise(splits[7], (HID,), 0.5, 3.0, (), jnp.float32)
    weight_mid = noise(splits[8], (HID, HID), HID ** -0.5, 0.25, (), jnp.float32)
    bias_mid = noise(splits[9], (HID,), 0.5, 3.0, (), jnp.float32)
    weight_out = noise(splits[10], (PCA, HID), HID ** -0.5, 0.25, (), jnp.float32)
    bias_out = noise(splits[11], (PCA,), 1.0, 4.0, (), jnp.float32)
    pca_basis = noise(splits[12], (NL, PCA), PCA ** -0.5, 0.75, ((0, 16),), jnp.float32)
    offset = noise(splits[13], (NL,), 1.0, 4.0, ((0, 16),), jnp.float32)
    return {"sources": sources, "bessel": bessel, "multipoles": multipoles, "window_low": window_low, "window_high": window_high, "params": params, "weight_in": weight_in, "bias_in": bias_in, "weight_mid": weight_mid, "bias_mid": bias_mid, "weight_out": weight_out, "bias_out": bias_out, "pca_basis": pca_basis, "offset": offset}


def primordial(params, window_low, window_high, first_wave, wave_count, total_waves):
    wave_index = first_wave + jnp.arange(wave_count, dtype=jnp.int32)
    log_ratio = math.log(0.002) + wave_index.astype(jnp.float32) * (math.log(5000.0) / total_waves)
    tilted = 0.5 * params[0][None, :] + 0.3 * params[1][None, :] * log_ratio[:, None]
    inside = (wave_index[:, None] >= window_low[None, :]) & (wave_index[:, None] < window_high[None, :])
    return jnp.where(inside, jnp.exp(tilted), jnp.zeros_like(tilted)) / total_waves


def silu_slope(value):
    sigma = jax.nn.sigmoid(value)
    return sigma * (1.0 + value * (1.0 - sigma))


def mat(left, right):
    return jnp.dot(left, right, precision=lax.Precision.HIGHEST)


def reference(sources, bessel, multipoles, window_low, window_high, params, weight_in, bias_in, weight_mid, bias_mid, weight_out, bias_out, pca_basis, offset):
    block_size = 16
    cosmos = params.shape[1]

    def accumulate(total, block_id):
        first_wave = block_id * block_size
        source_block = lax.dynamic_slice_in_dim(sources, first_wave, block_size, 1).astype(jnp.float32)
        kernel = lax.dynamic_slice_in_dim(bessel, first_wave, block_size, 0).astype(jnp.float32)
        transfer = jnp.einsum("tkc,ktl->klc", source_block, kernel, precision=lax.Precision.HIGHEST)
        factor = primordial(params, window_low, window_high, first_wave, block_size, NK)
        return total + jnp.einsum("klc,kc->lc", transfer * transfer, factor, precision=lax.Precision.HIGHEST), None

    power, _ = lax.scan(accumulate, jnp.zeros((NL, cosmos), jnp.float32), jnp.arange(NK // block_size, dtype=jnp.int32))
    degree = multipoles.astype(jnp.float32)
    smoothing = jnp.exp(-2.0 * degree * (degree + 1.0) / (LMAX * (LMAX + 1.0)))
    spectra = smoothing[:, None] * power

    inner_pre = mat(weight_in, params) + bias_in[:, None]
    inner_act = jax.nn.silu(inner_pre)
    middle_pre = mat(weight_mid, inner_act) + bias_mid[:, None]
    middle_act = jax.nn.silu(middle_pre)
    coeffs = mat(weight_out, middle_act) + bias_out[:, None]
    residual = offset[:, None] + mat(pca_basis, coeffs) - spectra
    grad_basis = mat(residual, coeffs.T) / cosmos
    coef_grad = mat(pca_basis.T, residual) / cosmos
    grad_weight_out = mat(coef_grad, middle_act.T)
    middle_delta = mat(weight_out.T, coef_grad) * silu_slope(middle_pre)
    grad_weight_mid = mat(middle_delta, inner_act.T)
    inner_delta = mat(weight_mid.T, middle_delta) * silu_slope(inner_pre)
    grad_weight_in = mat(inner_delta, params.T)
    return (spectra, grad_basis, grad_weight_in, grad_weight_mid, grad_weight_out)
```

```python
import functools
import math

import jax
import jax.numpy as jnp
from jax import lax
from jax.experimental import pallas as pl
from jax.experimental.pallas import tpu as pltpu
from jax.sharding import PartitionSpec as P

LMAX = 5000
LANES = 128
HIGHEST = lax.Precision.HIGHEST


def silu_slope(value):
    sigma = jax.nn.sigmoid(value)
    return sigma * (1.0 + value * (1.0 - sigma))


def mat(left, right, dims=((1,), (0,))):
    return lax.dot_general(
        left, right, (dims, ((), ())), precision=HIGHEST, preferred_element_type=jnp.float32
    )


def split_two(value):
    high = value.astype(jnp.bfloat16)
    low = (value - high.astype(jnp.float32)).astype(jnp.bfloat16)
    return high, low


def arrange_kernel(source_ref, extra_ref, *refs):
    *out_refs, rows_ref, turned_ref = refs
    times, cosmos, block = source_ref.shape
    packs = LANES // times
    low_count = cosmos // packs
    owners = out_refs[0].shape[0]
    extras = extra_ref.shape[0]
    rows_ref[...] = source_ref[...].astype(jnp.float32).reshape(times * cosmos, block)
    for low in range(low_count):
        pieces = [
            rows_ref[pl.ds(high * low_count + low, times, stride=cosmos), :]
            for high in range(packs)
        ]
        turned_ref[pl.ds(low, block, stride=low_count), :] = jnp.concatenate(pieces, axis=0).T
    turned = turned_ref[...].astype(jnp.bfloat16).reshape(owners, -1, low_count, LANES)
    start = 0
    for part, out_ref in enumerate(out_refs):
        last = part == len(out_refs) - 1
        waves = out_ref.shape[1] - (extras if last else 0)
        out_ref[:, :waves] = turned[:, start : start + waves]
        start += waves
    out_refs[-1][:, waves:] = jnp.broadcast_to(extra_ref[...][None], (owners,) + extra_ref.shape)


def arrange(sources, extra, chunks):
    times, cosmos, total = sources.shape
    low_count = cosmos // (LANES // times)
    block = LANES
    waves = sum(chunks)
    slots = chunks[:-1] + (chunks[-1] + extra.shape[0],)
    return pl.pallas_call(
        arrange_kernel,
        grid=(total // block,),
        in_specs=[
            pl.BlockSpec((times, cosmos, block), lambda b: (0, 0, b)),
            pl.BlockSpec(extra.shape, lambda b: (0, 0, 0)),
        ],
        out_specs=[
            pl.BlockSpec((block // waves, count, low_count, LANES), lambda b: (b, 0, 0, 0))
            for count in slots
        ],
        out_shape=[
            jax.ShapeDtypeStruct((total // waves, count, low_count, LANES), jnp.bfloat16)
            for count in slots
        ],
        scratch_shapes=[
            pltpu.VMEM((times * cosmos, block), jnp.float32),
            pltpu.VMEM((block * low_count, LANES), jnp.float32),
        ],
        compiler_params=pltpu.CompilerParams(vmem_limit_bytes=60 << 20),
        name="arrange",
    )(sources, extra)


def add_waves(total, first, received_ref, bessel_ref, column_refs, total_waves):
    first_param_ref, second_param_ref, low_ref, high_ref = column_refs
    peers, waves = received_ref.shape[:2]
    times = bessel_ref.shape[1] // peers
    packs = LANES // times
    for wave in range(waves):
        groups = []
        for group in range(peers // packs):
            tiles = [received_ref[group * packs + peer, wave] for peer in range(packs)]
            groups.append(
                jnp.concatenate(
                    [
                        jnp.concatenate(
                            [tile[:, high * times : (high + 1) * times] for tile in tiles], axis=1
                        )
                        for high in range(packs)
                    ],
                    axis=0,
                )
            )
        source = jnp.concatenate(groups, axis=1)
        transfer = jnp.dot(source, bessel_ref[wave], preferred_element_type=jnp.float32)
        index = first + wave
        log_ratio = math.log(0.002) + index.astype(jnp.float32) * (math.log(5000.0) / total_waves)
        tilted = 0.5 * first_param_ref[...] + 0.3 * second_param_ref[...] * log_ratio
        inside = (index >= low_ref[...]) & (index < high_ref[...])
        factor = jnp.where(inside, jnp.exp(tilted), jnp.zeros_like(tilted)) / total_waves
        total = total + transfer * transfer * factor
    return total


def power_kernel(total_waves, first_ref, received_ref, bessel_ref, *refs):
    *column_refs, power_ref = refs
    step = pl.program_id(0)

    @pl.when(step == 0)
    def _():
        power_ref[...] = jnp.zeros_like(power_ref)

    first = first_ref[0] + step * received_ref.shape[1]
    power_ref[...] = add_waves(
        power_ref[...], first, received_ref, bessel_ref, column_refs, total_waves
    )


def last_kernel(total_waves, owned, first_ref, received_ref, bessel_ref, *refs):
    *column_refs, extra_ref, base_ref, so_far_ref, out_ref, power_ref = refs
    step = pl.program_id(0)
    peers = received_ref.shape[0]
    cosmos, comps = base_ref.shape

    @pl.when(step == 0)
    def _():
        power_ref[...] = so_far_ref[...]

    first = first_ref[0] + step * received_ref.shape[1]
    total = add_waves(power_ref[...], first, received_ref, bessel_ref, column_refs, total_waves)
    power_ref[...] = total

    @pl.when(step == pl.num_programs(0) - 1)
    def _():
        power_high, power_low = split_two(total)
        extra = extra_ref[...].reshape(peers, -1, LANES)
        part = base_ref[...]
        basis = jnp.concatenate([extra[peer, :owned] for peer in range(peers)], axis=0)
        basis_high, basis_low = basis[:, :comps], basis[:, comps:]
        for left, right in (
            (power_low, basis_high),
            (power_high, basis_low),
            (power_high, basis_high),
        ):
            part = part - jnp.dot(left, right, preferred_element_type=jnp.float32)
        spare = jnp.zeros((cosmos, LANES - owned - comps), jnp.float32)
        for peer in range(peers):
            own = total[:, peer * owned : (peer + 1) * owned]
            out_ref[peer] = jnp.concatenate([own, part, spare], axis=1)


def power_parts(first, received, start, waves, bessel, columns, total_waves, owned, rest=None):
    peers, slots, low_count, _ = received.shape
    times, multipoles = bessel.shape[1:]
    cosmos = columns[0].shape[0]
    block = math.gcd(math.gcd(waves, start), 4)
    whole = lambda shape: pl.BlockSpec(shape, lambda s: (0,) * len(shape))
    in_specs = [
        pl.BlockSpec(memory_space=pltpu.SMEM),
        pl.BlockSpec((peers, block, low_count, LANES), lambda s: (0, s, 0, 0)),
        pl.BlockSpec((block, times, multipoles), lambda s: (start // block + s, 0, 0)),
    ] + [whole((cosmos, 1))] * len(columns)
    operands = [first + start, received, bessel, *columns]
    if rest is None:
        kernel = functools.partial(power_kernel, total_waves)
        out_shape = (cosmos, multipoles)
        scratch = []
    else:
        extras = slots - waves
        base, so_far = rest
        kernel = functools.partial(last_kernel, total_waves, owned)
        in_specs += [
            pl.BlockSpec((peers, extras, low_count, LANES), lambda s: (0, waves // extras, 0, 0)),
            whole(base.shape),
            whole(so_far.shape),
        ]
        operands += [received, base, so_far]
        out_shape = (peers, cosmos, LANES)
        scratch = [pltpu.VMEM((cosmos, multipoles), jnp.float32)]
    return pl.pallas_call(
        kernel,
        grid=(waves // block,),
        in_specs=in_specs,
        out_specs=whole(out_shape),
        out_shape=jax.ShapeDtypeStruct(out_shape, jnp.float32),
        scratch_shapes=scratch,
        compiler_params=pltpu.CompilerParams(vmem_limit_bytes=56 << 20),
        cost_estimate=pl.CostEstimate(
            flops=2 * waves * times * multipoles * cosmos,
            bytes_accessed=2 * waves * times * multipoles,
            transcendentals=0,
        ),
        name="power_parts",
    )(*operands)


def gradients_kernel(
    parts_ref,
    params_ref,
    coeffs_ref,
    inner_act_ref,
    inner_slope_ref,
    middle_act_ref,
    middle_slope_ref,
    weight_mid_ref,
    weight_out_ref,
    basis_ref,
    offset_ref,
    smoothing_ref,
    spectra_ref,
    grad_basis_ref,
    grad_in_ref,
    grad_mid_ref,
    grad_out_ref,
):
    cosmos = params_ref.shape[1]
    owned, comps = basis_ref.shape
    summed = jnp.sum(parts_ref[...], axis=0)
    spectra = summed[:, :owned] * smoothing_ref[...]
    coef_grad = summed[:, owned : owned + comps] / cosmos
    coeffs = coeffs_ref[...]
    residual = offset_ref[...] + mat(coeffs, basis_ref[...], ((1,), (1,))) - spectra
    middle_delta = mat(coef_grad, weight_out_ref[...]) * middle_slope_ref[...]
    inner_delta = mat(middle_delta, weight_mid_ref[...]) * inner_slope_ref[...]
    rows = ((0,), (0,))
    spectra_ref[...] = spectra.T
    grad_basis_ref[...] = mat(residual, coeffs, rows) / cosmos
    grad_out_ref[...] = mat(coef_grad, middle_act_ref[...], rows)
    grad_mid_ref[...] = mat(middle_delta, inner_act_ref[...], rows)
    grad_in_ref[...] = mat(params_ref[...], inner_delta)


def gradients(parts, params, coeffs, hidden, weight_mid, weight_out, basis, offset, smoothing):
    count, cosmos = params.shape
    owned, comps = basis.shape
    width = weight_mid.shape[0]
    shape = lambda *dims: jax.ShapeDtypeStruct(dims, jnp.float32)
    return pl.pallas_call(
        gradients_kernel,
        out_shape=(
            shape(owned, cosmos),
            shape(owned, comps),
            shape(count, width),
            shape(width, width),
            shape(comps, width),
        ),
        compiler_params=pltpu.CompilerParams(vmem_limit_bytes=48 << 20),
        name="gradients",
    )(
        parts,
        params,
        coeffs,
        *hidden,
        weight_mid,
        weight_out,
        basis,
        offset.reshape(1, owned),
        smoothing.reshape(1, owned),
    )


def local(
    sources,
    bessel,
    multipoles,
    window_low,
    window_high,
    params,
    weight_in,
    bias_in,
    weight_mid,
    bias_mid,
    weight_out,
    bias_out,
    pca_basis,
    offset,
):
    waves = bessel.shape[0]
    total_waves = sources.shape[1]
    peers = total_waves // waves
    cosmos = params.shape[1]
    owned = multipoles.shape[0]

    degree = multipoles.astype(jnp.float32)
    smoothing = jnp.exp(-2.0 * degree * (degree + 1.0) / (LMAX * (LMAX + 1.0)))
    low_count = cosmos // (LANES // sources.shape[0])
    smooth_basis = smoothing[:, None] * pca_basis
    rounded = lax.reduce_precision(smooth_basis, exponent_bits=8, mantissa_bits=7)
    smooth_basis = jnp.concatenate([rounded, smooth_basis - rounded], axis=1).astype(jnp.bfloat16)
    smooth_basis = jnp.pad(smooth_basis, ((0, -owned % low_count), (0, 0)))
    extra = smooth_basis.reshape(-1, low_count, LANES)

    chunks = (waves - waves // 4, waves // 4)
    ready = arrange(jnp.transpose(sources, (0, 2, 1)), extra, chunks)
    received = [
        lax.all_to_all(part, "ka", split_axis=0, concat_axis=0, tiled=True) for part in ready
    ]

    inner_pre = mat(params.T, weight_in.T) + bias_in[None, :]
    inner_act = jax.nn.silu(inner_pre)
    middle_pre = mat(inner_act, weight_mid.T) + bias_mid[None, :]
    middle_act = jax.nn.silu(middle_pre)
    coeffs = mat(middle_act, weight_out.T) + bias_out[None, :]
    hidden = (inner_act, silu_slope(inner_pre), middle_act, silu_slope(middle_pre))
    base = mat(offset[None, :] + mat(coeffs, pca_basis.T), pca_basis)

    first = (lax.axis_index("ka") * waves).astype(jnp.int32).reshape(1)
    columns = [row.reshape(cosmos, 1) for row in (params[0], params[1], window_low, window_high)]
    power = power_parts(first, received[0], 0, chunks[0], bessel, columns, total_waves, owned)
    parts = power_parts(
        first,
        received[1],
        chunks[0],
        chunks[1],
        bessel,
        columns,
        total_waves,
        owned,
        (base, power),
    )
    gathered = lax.all_to_all(parts, "ka", split_axis=0, concat_axis=0, tiled=True)
    spectra, grad_basis, grad_in, grad_mid, grad_out = gradients(
        gathered, params, coeffs, hidden, weight_mid, weight_out, pca_basis, offset, smoothing
    )
    return (spectra, grad_basis, grad_in.T, grad_mid, grad_out)


def solution(mesh):
    return jax.shard_map(
        local,
        mesh=mesh,
        in_specs=(
            P("ka", None, "grp"),
            P("ka", None, None),
            P("ka"),
            P("grp"),
            P("grp"),
            P(None, "grp"),
            P(),
            P(),
            P(),
            P(),
            P(),
            P(),
            P("ka", None),
            P("ka"),
        ),
        out_specs=(
            P("ka", "grp"),
            P(("grp", "ka"), None),
            P("grp", None),
            P("grp", None),
            P("grp", None),
        ),
        check_vma=False,
    )
```

```python
import functools
import math

import jax
import jax.numpy as jnp
from jax import lax
from jax.experimental import pallas as pl
from jax.experimental.pallas import tpu as pltpu
from jax.sharding import PartitionSpec as P

LMAX = 5000
LANES = 128
TOPS = (2, 1, 0, 3)
HIGHEST = lax.Precision.HIGHEST


def silu_slope(value):
    sigma = jax.nn.sigmoid(value)
    return sigma * (1.0 + value * (1.0 - sigma))


def mat(left, right, dims=((1,), (0,))):
    return lax.dot_general(
        left, right, (dims, ((), ())), precision=HIGHEST, preferred_element_type=jnp.float32
    )


def split_two(value):
    high = value.astype(jnp.bfloat16)
    low = (value - high.astype(jnp.float32)).astype(jnp.bfloat16)
    return high, low


def smoothing_of(multipoles):
    degree = multipoles.astype(jnp.float32)
    return jnp.exp(-2.0 * degree * (degree + 1.0) / (LMAX * (LMAX + 1.0)))


def column(row):
    return jnp.broadcast_to(row.astype(jnp.float32), (8, row.shape[1])).T[:, :1]


def smooth_basis(multipoles_ref, basis_ref, low_count):
    value = column(smoothing_of(multipoles_ref[...])) * basis_ref[...]
    value = jnp.concatenate([part.astype(jnp.float32) for part in split_two(value)], axis=1)
    spare = -value.shape[0] % low_count
    if spare:
        value = jnp.concatenate([value, jnp.zeros((spare, LANES), jnp.float32)], axis=0)
    return value.astype(jnp.bfloat16).reshape(-1, low_count, LANES)


def arrange_kernel(group, last, waves, source_ref, multipoles_ref, basis_ref, *refs):
    *out_refs, block_ref, rows_ref, turned_ref, sems = refs
    blocks, times, cosmos, block = block_ref.shape
    packs = LANES // times
    low_count = cosmos // packs
    size = waves * low_count
    me = lax.axis_index("ka")
    copies = []
    for slot, top in enumerate(TOPS):
        start = pl.multiple_of(((me // group) ^ top) * block, block)
        copy = pltpu.make_async_copy(
            source_ref.at[:, :, pl.ds(start, block)], block_ref.at[slot], sems.at[slot]
        )
        copy.start()
        copies.append(copy)
    extra = smooth_basis(multipoles_ref, basis_ref, low_count)
    for slot, copy in enumerate(copies):
        copy.wait()
        rows_ref[...] = block_ref[slot].astype(jnp.float32).reshape(times * cosmos, block)
        for low in range(low_count):
            pieces = [
                rows_ref[pl.ds(high * low_count + low, times, stride=cosmos), :]
                for high in range(packs)
            ]
            turned_ref[pl.ds(low, block, stride=low_count), :] = jnp.concatenate(pieces, axis=0).T
        for peer in range(group):
            start = pl.multiple_of((peer ^ (me % group)) * size, size)
            piece = turned_ref[pl.ds(start, size), :].astype(jnp.bfloat16)
            piece = piece.reshape(waves, low_count, LANES)
            chip, core = TOPS[slot] * group // 2 + peer // 2, peer % 2
            if chip in (0, last):
                out_ref = out_refs[-1].at[int(chip == last)] if core else out_refs[chip]
                out_ref[:waves] = piece
                out_ref[waves:] = extra
            else:
                out_refs[chip][core * waves : (core + 1) * waves] = piece
                out_refs[chip][2 * waves :] = extra


def arrange(sources, multipoles, basis, waves, group, last):
    times, cosmos, total = sources.shape
    low_count = cosmos // (LANES // times)
    block = waves * group
    extras = -(-basis.shape[0] // low_count)
    one, two = (count * waves + extras for count in (1, 2))
    chips = total // waves // 2
    shapes = [(one if chip in (0, last) else two, low_count, LANES) for chip in range(chips)]
    shapes.append((2, one, low_count, LANES))
    vmem = pl.BlockSpec(memory_space=pltpu.VMEM)
    return pl.pallas_call(
        functools.partial(arrange_kernel, group, last, waves),
        in_specs=[pl.BlockSpec(memory_space=pl.ANY), vmem, vmem],
        out_specs=[vmem] * len(shapes),
        out_shape=[jax.ShapeDtypeStruct(shape, jnp.bfloat16) for shape in shapes],
        scratch_shapes=[
            pltpu.VMEM((len(TOPS), times, cosmos, block), jnp.bfloat16),
            pltpu.VMEM((times * cosmos, block), jnp.float32),
            pltpu.VMEM((block * low_count, LANES), jnp.float32),
            pltpu.SemaphoreType.DMA((len(TOPS),)),
        ],
        compiler_params=pltpu.CompilerParams(vmem_limit_bytes=24 << 20),
        cost_estimate=pl.CostEstimate(
            flops=0, bytes_accessed=16 * times * cosmos * total, transcendentals=0
        ),
        name="arrange",
    )(sources, multipoles, basis)


def source_rows(stage_ref, wave, times):
    tiles = [stage_ref[peer, wave] for peer in range(stage_ref.shape[0])]
    rows = [
        jnp.concatenate([tile[:, start : start + times] for tile in tiles], axis=1)
        for start in range(0, LANES, times)
    ]
    return jnp.concatenate(rows, axis=0)


def transfer_kernel(group, chips, times, me_ref, *refs):
    count = len(chips) * 2
    pieces, extras, refs = refs[:count], refs[count : 2 * count], refs[2 * count :]
    *bessel_refs, whole_ref, out_ref, held_ref, basis_ref, stage_ref, sem = refs
    me = me_ref[0]
    span = held_ref.shape[1]
    start = pl.multiple_of(((me // group) ^ TOPS[-1]) * span, span)
    copy = pltpu.make_async_copy(whole_ref.at[:, pl.ds(start, span), :], held_ref, sem)
    step = pl.program_id(0)

    @pl.when(step == 0)
    def _():
        copy.start()
        for number, extra_ref in enumerate(extras):
            apart = chips[number // 2] * 2 + number % 2
            basis_ref[apart] = extra_ref[...].reshape(basis_ref.shape[1:])

    for number in range(count):
        stage_ref[number // group, (number % group) ^ (me % group)] = pieces[number][...]
    for wave in range(out_ref.shape[0]):
        total = None
        for number, bessel_ref in enumerate(bessel_refs):
            part = jnp.dot(
                source_rows(stage_ref.at[number], wave, times),
                bessel_ref[wave],
                preferred_element_type=jnp.float32,
            )
            total = part if total is None else total + part
        out_ref[wave] = total
    pl.when(step == pl.num_programs(0) - 1)(copy.wait)


def tiles_spec(array, lead, start, size, moves):
    rest = array.shape[-2:]
    index = lambda s, me: (start // size + s * moves, 0, 0)
    if lead is None:
        return pl.BlockSpec((size,) + rest, index)
    return pl.BlockSpec((None, size) + rest, lambda s, me: (lead,) + index(s, me))


def add_groups(me, group, chips, members, bessel, times, extras):
    low_count = members[0][0].shape[-2]
    waves, _, multipoles = bessel.shape
    cosmos = low_count * (LANES // times)
    block = math.gcd(waves, 8)
    in_specs = [tiles_spec(array, lead, at, block, 1) for array, lead, at, _ in members]
    in_specs += [tiles_spec(array, lead, at, extras, 0) for array, lead, _, at in members]

    span = group * times
    in_specs += [
        pl.BlockSpec((block, span, multipoles), lambda s, me, top=top: (s, (me[0] // group) ^ top, 0))
        for top in TOPS[:-1]
    ]
    in_specs.append(pl.BlockSpec(memory_space=pl.ANY))
    arrays = [member[0] for member in members]
    basis = (len(members) + group, extras * low_count, LANES)
    return pl.pallas_call(
        functools.partial(transfer_kernel, group, chips, times),
        grid_spec=pltpu.PrefetchScalarGridSpec(
            num_scalar_prefetch=1,
            grid=(waves // block,),
            in_specs=in_specs,
            out_specs=[
                pl.BlockSpec((block, cosmos, multipoles), lambda s, me: (s, 0, 0)),
                pl.BlockSpec(memory_space=pltpu.VMEM),
                pl.BlockSpec(basis, lambda s, me: (0, 0, 0)),
            ],
            scratch_shapes=[
                pltpu.VMEM((len(TOPS) - 1, group, block, low_count, LANES), jnp.bfloat16),
                pltpu.SemaphoreType.DMA,
            ],
        ),
        out_shape=[
            jax.ShapeDtypeStruct((waves, cosmos, multipoles), jnp.float32),
            jax.ShapeDtypeStruct((waves, span, multipoles), bessel.dtype),
            jax.ShapeDtypeStruct(basis, jnp.bfloat16),
        ],
        compiler_params=pltpu.CompilerParams(vmem_limit_bytes=24 << 20),
        cost_estimate=pl.CostEstimate(
            flops=16 * math.prod(bessel.shape) * cosmos,
            bytes_accessed=2 * math.prod(bessel.shape),
            transcendentals=0,
        ),
        name="transfer",
    )(me, *arrays, *arrays, *[bessel] * len(TOPS))


def power_kernel(times, chips, total_waves, *refs):
    piece_refs, traded_ref, held_ref, rest_ref, *refs = refs[: len(chips)], *refs[len(chips) :]
    params_ref, low_ref, high_ref, basis_ref, base_ref, out_ref, stage_ref, all_ref = refs
    waves, cosmos, multipoles = rest_ref.shape
    comps = base_ref.shape[1]
    peers = all_ref.shape[0]
    owned = multipoles // peers
    group = 2 * len(chips)
    extras = traded_ref.shape[1] - waves
    me = lax.axis_index("ka")
    all_ref[...] = basis_ref[...]
    for low, (chip, piece_ref) in enumerate(zip(chips, piece_refs)):
        joined = low == len(chips) - 1
        for core in range(2):
            if core and not joined:
                piece, extra = traded_ref[low, :waves], traded_ref[low, waves:]
            else:
                start = 2 * waves + core * extras
                piece, extra = piece_ref[core * waves : (core + 1) * waves], piece_ref[start : start + extras]
            stage_ref[(2 * low + core) ^ (me % group)] = piece
            all_ref[2 * chip + core] = extra.reshape(all_ref.shape[1:])
    first_param, second_param = column(params_ref[0:1]), column(params_ref[1:2])
    low, high = column(low_ref[...]), column(high_ref[...])
    total = jnp.zeros((cosmos, multipoles), jnp.float32)
    for wave in range(waves):
        transfer = rest_ref[wave] + jnp.dot(
            source_rows(stage_ref, wave, times),
            held_ref[wave],
            preferred_element_type=jnp.float32,
        )
        index = (me * waves + wave).astype(jnp.float32)
        log_ratio = math.log(0.002) + index * (math.log(5000.0) / total_waves)
        tilted = 0.5 * first_param + 0.3 * second_param * log_ratio
        inside = (index >= low) & (index < high)
        factor = jnp.where(inside, jnp.exp(tilted), jnp.zeros_like(tilted)) / total_waves
        total = total + transfer * transfer * factor

    basis = jnp.concatenate([all_ref[peer ^ me][:owned] for peer in range(peers)], axis=0)
    power_high, power_low = split_two(total)
    basis_high, basis_low = basis[:, :comps], basis[:, comps:]
    part = base_ref[...]
    for left, right in (
        (power_low, basis_high),
        (power_high, basis_low),
        (power_high, basis_high),
    ):
        part = part - jnp.dot(left, right, preferred_element_type=jnp.float32)
    for peer in range(peers):
        own = total[:, peer * owned : (peer + 1) * owned]
        out_ref[peer] = fold(jnp.concatenate([own, part], axis=1))


def power_parts(pieces, traded, held, rest, times, chips, total_waves, extra):
    low_count = traded.shape[2]
    waves, cosmos, multipoles = rest.shape
    basis, base = extra[-2:]
    peers = basis.shape[0]
    operands = [*pieces, traded, held, rest, *extra]
    rows = folded_rows(cosmos, multipoles // peers + base.shape[1])
    return pl.pallas_call(
        functools.partial(power_kernel, times, chips, total_waves),
        in_specs=[pl.BlockSpec(memory_space=pltpu.VMEM)] * len(operands),
        out_specs=pl.BlockSpec(memory_space=pltpu.VMEM),
        out_shape=jax.ShapeDtypeStruct((peers, rows, LANES), jnp.float32),
        scratch_shapes=[
            pltpu.VMEM((2 * len(chips), waves, low_count, LANES), jnp.bfloat16),
            pltpu.VMEM(basis.shape, jnp.bfloat16),
        ],
        compiler_params=pltpu.CompilerParams(vmem_limit_bytes=24 << 20),
        cost_estimate=pl.CostEstimate(
            flops=16 * waves * held.shape[1] * multipoles * cosmos,
            bytes_accessed=2 * waves * held.shape[1] * multipoles,
            transcendentals=0,
        ),
        name="power",
    )(*operands)


def folds(rows, width):
    spare = LANES - width
    strips = width // spare if spare and width % spare == 0 else 0
    return strips if rows % (8 * (strips + 1)) == 0 else 0


def fold(value):
    rows, width = value.shape
    strips = folds(rows, width)
    if not strips:
        return jnp.concatenate([value, jnp.zeros((rows, LANES - width), value.dtype)], axis=1)
    spare = LANES - width
    head = rows * strips // (strips + 1)
    tail = [value[head:, strip * spare : (strip + 1) * spare] for strip in range(strips)]
    return jnp.concatenate([value[:head], jnp.concatenate(tail, axis=0)], axis=1)


def unfold(value, rows, width):
    strips = folds(rows, width)
    if not strips:
        return value[:, :width]
    size = rows // (strips + 1)
    tail = [value[strip * size : (strip + 1) * size, width:] for strip in range(strips)]
    return jnp.concatenate([value[:, :width], jnp.concatenate(tail, axis=1)], axis=0)


def folded_rows(rows, width):
    strips = folds(rows, width)
    return rows * strips // (strips + 1) if strips else rows


def gradients_kernel(
    parts_ref,
    params_ref,
    coeffs_ref,
    inner_act_ref,
    inner_slope_ref,
    middle_act_ref,
    middle_slope_ref,
    weight_mid_ref,
    weight_out_ref,
    basis_ref,
    offset_ref,
    multipoles_ref,
    spectra_ref,
    grad_basis_ref,
    grad_in_ref,
    grad_mid_ref,
    grad_out_ref,
):
    cosmos = params_ref.shape[1]
    owned, comps = basis_ref.shape
    summed = unfold(jnp.sum(parts_ref[...], axis=0), cosmos, owned + comps)
    spectra = summed[:, :owned] * smoothing_of(multipoles_ref[...])
    coef_grad = summed[:, owned : owned + comps] / cosmos
    coeffs = coeffs_ref[...]
    residual = offset_ref[...] + mat(coeffs, basis_ref[...], ((1,), (1,))) - spectra
    middle_delta = mat(coef_grad, weight_out_ref[...]) * middle_slope_ref[...]
    inner_delta = mat(middle_delta, weight_mid_ref[...]) * inner_slope_ref[...]
    rows = ((0,), (0,))
    spectra_ref[...] = spectra.T
    grad_basis_ref[...] = mat(residual, coeffs, rows) / cosmos
    grad_out_ref[...] = mat(coef_grad, middle_act_ref[...], rows)
    grad_mid_ref[...] = mat(middle_delta, inner_act_ref[...], rows)
    grad_in_ref[...] = mat(params_ref[...], inner_delta)


def gradients(parts, params, coeffs, hidden, weight_mid, weight_out, basis, offset, multipoles):
    count, cosmos = params.shape
    owned, comps = basis.shape
    width = weight_mid.shape[0]
    shape = lambda *dims: jax.ShapeDtypeStruct(dims, jnp.float32)
    return pl.pallas_call(
        gradients_kernel,
        out_shape=(
            shape(owned, cosmos),
            shape(owned, comps),
            shape(count, width),
            shape(width, width),
            shape(comps, width),
        ),
        compiler_params=pltpu.CompilerParams(vmem_limit_bytes=48 << 20),
        name="gradients",
    )(
        parts,
        params,
        coeffs,
        *hidden,
        weight_mid,
        weight_out,
        basis,
        offset.reshape(1, owned),
        multipoles,
    )


def exchange(value, apart, peers):
    return lax.ppermute(value, "ka", [(peer, peer ^ apart) for peer in range(peers)])


def after(value, *others):
    return lax.optimization_barrier((value, *others))[0]


def local(
    sources,
    bessel,
    multipoles,
    window_low,
    window_high,
    params,
    weight_in,
    bias_in,
    weight_mid,
    bias_mid,
    weight_out,
    bias_out,
    pca_basis,
    offset,
):
    waves = bessel.shape[0]
    total_waves = sources.shape[1]
    peers = total_waves // waves
    cosmos = params.shape[1]
    owned = multipoles.shape[0]
    group = LANES // waves
    half = group // 2
    times = sources.shape[0]
    extras = -(-owned // (cosmos * times // LANES))
    me = lax.axis_index("ka").astype(jnp.int32).reshape(1)
    own_multipoles = multipoles.reshape(1, owned)
    turned = jnp.transpose(sources, (0, 2, 1))

    chips = [top * half + low for top in TOPS for low in range(half)]
    late, last = chips[-half:], chips[-1]
    *ready, give = arrange(turned, own_multipoles, pca_basis, waves, group, last)
    given = exchange(give, 1, peers)
    got = {}
    near = [chip for chip in chips if 0 < chip < half]
    for chip in chips:
        if chip in (0, last):
            continue
        value = ready[chip]
        if chip in near:
            value = after(value, got[half + near.index(chip)])
        got[chip] = exchange(value, 2 * chip, peers)
    mine, other = ready[last], given[1]
    value = jnp.concatenate([mine[:waves], other[:waves], mine[waves:], other[waves:]])
    got[last] = exchange(value, 2 * last, peers)

    others = lambda part, *then: jnp.stack([after(got[chip], *then)[waves:] for chip in part])
    early = [chip for chip in chips[:-half] if chip]
    traded = exchange(others(early), 1, peers)
    members = []
    for chip in chips[:-half]:
        if chip:
            members += [(got[chip], None, 0, 2 * waves), (traded, early.index(chip), 0, waves)]
        else:
            members += [(ready[0], None, 0, waves), (given, 0, 0, waves)]
    rest, held, basis = add_groups(me, group, chips[:-half], members, bessel, times, extras)
    late_traded = exchange(others(late[:-1], rest), 1, peers)

    inner_pre = mat(params.T, weight_in.T) + bias_in[None, :]
    inner_act = jax.nn.silu(inner_pre)
    middle_pre = mat(inner_act, weight_mid.T) + bias_mid[None, :]
    middle_act = jax.nn.silu(middle_pre)
    coeffs = mat(middle_act, weight_out.T) + bias_out[None, :]
    hidden = (inner_act, silu_slope(inner_pre), middle_act, silu_slope(middle_pre))
    base = mat(offset[None, :] + mat(coeffs, pca_basis.T), pca_basis)

    extra = (params, window_low.reshape(1, cosmos), window_high.reshape(1, cosmos), basis, base)
    pieces = [got[chip] for chip in late]
    parts = power_parts(pieces, late_traded, held, rest, times, late, total_waves, extra)
    gathered = lax.all_to_all(parts, "ka", split_axis=0, concat_axis=0, tiled=True)
    spectra, grad_basis, grad_in, grad_mid, grad_out = gradients(
        gathered, params, coeffs, hidden, weight_mid, weight_out, pca_basis, offset, own_multipoles
    )
    return (spectra, grad_basis, grad_in.T, grad_mid, grad_out)


def solution(mesh):
    return jax.shard_map(
        local,
        mesh=mesh,
        in_specs=(
            P("ka", None, "grp"),
            P("ka", None, None),
            P("ka"),
            P("grp"),
            P("grp"),
            P(None, "grp"),
            P(),
            P(),
            P(),
            P(),
            P(),
            P(),
            P("ka", None),
            P("ka"),
        ),
        out_specs=(
            P("ka", "grp"),
            P(("grp", "ka"), None),
            P("grp", None),
            P("grp", None),
            P("grp", None),
        ),
        check_vma=False,
    )
```

```python
import functools
import math

import jax
import jax.numpy as jnp
from jax import lax
from jax.experimental import pallas as pl
from jax.experimental.pallas import tpu as pltpu
from jax.sharding import PartitionSpec as P

LMAX = 5000
LANES = 128
TOPS = (2, 1, 0, 3)
HELD = (3,)
FIRST = 2
HIGHEST = lax.Precision.HIGHEST


def silu_slope(value):
    sigma = jax.nn.sigmoid(value)
    return sigma * (1.0 + value * (1.0 - sigma))


def mat(left, right, dims=((1,), (0,))):
    return lax.dot_general(
        left, right, (dims, ((), ())), precision=HIGHEST, preferred_element_type=jnp.float32
    )


def split_two(value):
    high = value.astype(jnp.bfloat16)
    low = (value - high.astype(jnp.float32)).astype(jnp.bfloat16)
    return high, low


def smoothing_of(multipoles):
    degree = multipoles.astype(jnp.float32)
    return jnp.exp(-2.0 * degree * (degree + 1.0) / (LMAX * (LMAX + 1.0)))


def column(row):
    return jnp.broadcast_to(row.astype(jnp.float32), (8, row.shape[1])).T[:, :1]


def smooth_basis(multipoles_ref, basis_ref, low_count):
    value = column(smoothing_of(multipoles_ref[...])) * basis_ref[...]
    value = jnp.concatenate([part.astype(jnp.float32) for part in split_two(value)], axis=1)
    spare = -value.shape[0] % low_count
    if spare:
        value = jnp.concatenate([value, jnp.zeros((spare, LANES), jnp.float32)], axis=0)
    return value.astype(jnp.bfloat16).reshape(-1, low_count, LANES)


def arrange_kernel(tops, group, last, waves, held_tops, source_ref, *refs):
    multipoles_ref, basis_ref, whole_ref, *refs = refs
    held_refs, refs = refs[: len(held_tops)], refs[len(held_tops) :]
    *out_refs, block_ref, rows_ref, turned_ref, sems, held_sems = refs
    _, times, cosmos, block = block_ref.shape
    packs = LANES // times
    low_count = cosmos // packs
    size = waves * low_count
    me = lax.axis_index("ka")
    copies = []
    for slot, top in enumerate(tops):
        start = pl.multiple_of(((me // group) ^ top) * block, block)
        copy = pltpu.make_async_copy(
            source_ref.at[:, :, pl.ds(start, block)], block_ref.at[slot], sems.at[slot]
        )
        copy.start()
        copies.append(copy)
    holds = []
    for slot, (top, held_ref) in enumerate(zip(held_tops, held_refs)):
        span = group * times
        start = pl.multiple_of(((me // group) ^ top) * span, span)
        copy = pltpu.make_async_copy(
            whole_ref.at[:, pl.ds(start, span), :], held_ref, held_sems.at[slot]
        )
        copy.start()
        holds.append(copy)
    extra = smooth_basis(multipoles_ref, basis_ref, low_count)
    chips = [top * group // 2 + low for top in tops for low in range(group // 2)]
    for slot, copy in enumerate(copies):
        copy.wait()
        rows_ref[...] = block_ref[slot].astype(jnp.float32).reshape(times * cosmos, block)
        for low in range(low_count):
            pieces = [
                rows_ref[pl.ds(high * low_count + low, times, stride=cosmos), :]
                for high in range(packs)
            ]
            turned_ref[pl.ds(low, block, stride=low_count), :] = jnp.concatenate(pieces, axis=0).T
        for peer in range(group):
            start = pl.multiple_of((peer ^ (me % group)) * size, size)
            piece = turned_ref[pl.ds(start, size), :].astype(jnp.bfloat16)
            piece = piece.reshape(waves, low_count, LANES)
            chip, core = tops[slot] * group // 2 + peer // 2, peer % 2
            out_ref = out_refs[chips.index(chip)]
            if chip in (0, last):
                out_ref = out_refs[-1].at[int(chip == last)] if core else out_ref
                out_ref[:waves] = piece
                out_ref[waves:] = extra
            else:
                out_ref[core * waves : (core + 1) * waves] = piece
                out_ref[2 * waves :] = extra
    for copy in holds:
        copy.wait()


def arrange(sources, multipoles, basis, bessel, tops, group, last, held_tops=()):
    times, cosmos, total = sources.shape
    waves, _, multipole_count = bessel.shape
    low_count = cosmos // (LANES // times)
    block = waves * group
    extras = -(-basis.shape[0] // low_count)
    one, two = (count * waves + extras for count in (1, 2))
    chips = [top * group // 2 + low for top in tops for low in range(group // 2)]
    shapes = [(one if chip in (0, last) else two, low_count, LANES) for chip in chips]
    if last in chips:
        shapes.append((2, one, low_count, LANES))
    held = pltpu.VMEM((waves, group * times, multipole_count), bessel.dtype)
    vmem, anywhere = (pl.BlockSpec(memory_space=space) for space in (pltpu.VMEM, pl.ANY))
    return pl.pallas_call(
        functools.partial(arrange_kernel, tops, group, last, waves, held_tops),
        in_specs=[anywhere, vmem, vmem, anywhere],
        out_specs=[vmem] * (len(held_tops) + len(shapes)),
        out_shape=[held] * len(held_tops)
        + [jax.ShapeDtypeStruct(shape, jnp.bfloat16) for shape in shapes],
        scratch_shapes=[
            pltpu.VMEM((len(tops), times, cosmos, block), jnp.bfloat16),
            pltpu.VMEM((times * cosmos, block), jnp.float32),
            pltpu.VMEM((block * low_count, LANES), jnp.float32),
            pltpu.SemaphoreType.DMA((len(tops),)),
            pltpu.SemaphoreType.DMA((max(1, len(held_tops)),)),
        ],
        compiler_params=pltpu.CompilerParams(vmem_limit_bytes=(50 if held_tops else 61) << 20),
        cost_estimate=pl.CostEstimate(
            flops=0, bytes_accessed=16 * times * cosmos * block * len(tops), transcendentals=0
        ),
        name="arrange",
    )(sources, multipoles, basis, bessel)


def source_rows(stage_ref, wave, times):
    tiles = [stage_ref[peer, wave] for peer in range(stage_ref.shape[0])]
    rows = [
        jnp.concatenate([tile[:, start : start + times] for tile in tiles], axis=1)
        for start in range(0, LANES, times)
    ]
    return jnp.concatenate(rows, axis=0)


def transfer_kernel(group, members, times, me_ref, *refs):
    count = 1 + max(member[1] for member in members)
    arrays, (*bessel_refs, out_ref, basis_ref, stage_ref) = refs[:count], refs[count:]
    me = me_ref[0]
    step = pl.program_id(0)
    waves = out_ref.shape[0]
    extras = basis_ref.shape[1] // stage_ref.shape[3]

    def tiles(array, lead, rows):
        return arrays[array][rows] if lead is None else arrays[array][lead, rows]

    @pl.when(step == 0)
    def _():
        for apart, array, lead, _, at in members:
            extra = tiles(array, lead, pl.ds(at, extras))
            basis_ref[apart] = extra.reshape(basis_ref.shape[1:])

    for number, (_, array, lead, at, _) in enumerate(members):
        place = (number % group) ^ (me % group)
        stage_ref[number // group, place] = tiles(array, lead, pl.ds(at + step * waves, waves))
    for wave in range(waves):
        total = None
        for number, bessel_ref in enumerate(bessel_refs):
            part = jnp.dot(
                source_rows(stage_ref.at[number], wave, times),
                bessel_ref[wave],
                preferred_element_type=jnp.float32,
            )
            total = part if total is None else total + part
        out_ref[wave] = total


def add_groups(me, group, arrays, members, bessel, times, extras):
    low_count = arrays[0].shape[-2]
    waves, _, multipoles = bessel.shape
    span = group * times
    cosmos = low_count * (LANES // times)
    block = math.gcd(waves, 8)
    in_specs = [pl.BlockSpec(memory_space=pltpu.VMEM)] * len(arrays)
    in_specs += [
        pl.BlockSpec(
            (block, span, multipoles), lambda s, me, top=top: (s, (me[0] // group) ^ top, 0)
        )
        for top in TOPS[:-1]
    ]
    basis = (len(members) + group, extras * low_count, LANES)
    return pl.pallas_call(
        functools.partial(transfer_kernel, group, members, times),
        grid_spec=pltpu.PrefetchScalarGridSpec(
            num_scalar_prefetch=1,
            grid=(waves // block,),
            in_specs=in_specs,
            out_specs=[
                pl.BlockSpec((block, cosmos, multipoles), lambda s, me: (s, 0, 0)),
                pl.BlockSpec(basis, lambda s, me: (0, 0, 0)),
            ],
            scratch_shapes=[
                pltpu.VMEM((len(TOPS) - 1, group, block, low_count, LANES), jnp.bfloat16),
            ],
        ),
        out_shape=[
            jax.ShapeDtypeStruct((waves, cosmos, multipoles), jnp.float32),
            jax.ShapeDtypeStruct(basis, jnp.bfloat16),
        ],
        compiler_params=pltpu.CompilerParams(vmem_limit_bytes=24 << 20),
        cost_estimate=pl.CostEstimate(
            flops=16 * math.prod(bessel.shape) * cosmos,
            bytes_accessed=2 * math.prod(bessel.shape),
            transcendentals=0,
        ),
        name="transfer",
    )(me, *arrays, *[bessel] * (len(TOPS) - 1))


def power_kernel(times, chips, total_waves, *refs):
    piece_refs, traded_ref, held_ref, rest_ref, *refs = refs[: len(chips)], *refs[len(chips) :]
    params_ref, low_ref, high_ref, basis_ref, base_ref, out_ref, stage_ref, all_ref = refs
    waves, cosmos, multipoles = rest_ref.shape
    comps = base_ref.shape[1]
    peers = all_ref.shape[0]
    owned = multipoles // peers
    group = 2 * len(chips)
    extras = traded_ref.shape[1] - waves
    me = lax.axis_index("ka")
    all_ref[...] = basis_ref[...]
    for low, (chip, piece_ref) in enumerate(zip(chips, piece_refs)):
        joined = low == len(chips) - 1
        for core in range(2):
            if core and not joined:
                piece, extra = traded_ref[low, :waves], traded_ref[low, waves:]
            else:
                start = 2 * waves + core * extras
                piece, extra = piece_ref[core * waves : (core + 1) * waves], piece_ref[start : start + extras]
            stage_ref[(2 * low + core) ^ (me % group)] = piece
            all_ref[2 * chip + core] = extra.reshape(all_ref.shape[1:])
    first_param, second_param = column(params_ref[0:1]), column(params_ref[1:2])
    low, high = column(low_ref[...]), column(high_ref[...])
    total = jnp.zeros((cosmos, multipoles), jnp.float32)
    for wave in range(waves):
        transfer = rest_ref[wave] + jnp.dot(
            source_rows(stage_ref, wave, times),
            held_ref[wave],
            preferred_element_type=jnp.float32,
        )
        index = (me * waves + wave).astype(jnp.float32)
        log_ratio = math.log(0.002) + index * (math.log(5000.0) / total_waves)
        tilted = 0.5 * first_param + 0.3 * second_param * log_ratio
        inside = (index >= low) & (index < high)
        factor = jnp.where(inside, jnp.exp(tilted), jnp.zeros_like(tilted)) / total_waves
        total = total + transfer * transfer * factor

    basis = jnp.concatenate([all_ref[peer ^ me][:owned] for peer in range(peers)], axis=0)
    power_high, power_low = split_two(total)
    basis_high, basis_low = basis[:, :comps], basis[:, comps:]
    part = base_ref[...]
    for left, right in (
        (power_low, basis_high),
        (power_high, basis_low),
        (power_high, basis_high),
    ):
        part = part - jnp.dot(left, right, preferred_element_type=jnp.float32)
    for peer in range(peers):
        own = total[:, peer * owned : (peer + 1) * owned]
        out_ref[peer] = fold(jnp.concatenate([own, part], axis=1))


def power_parts(pieces, traded, held, rest, times, chips, total_waves, extra):
    low_count = traded.shape[2]
    waves, cosmos, multipoles = rest.shape
    basis, base = extra[-2:]
    peers = basis.shape[0]
    operands = [*pieces, traded, held, rest, *extra]
    rows = folded_rows(cosmos, multipoles // peers + base.shape[1])
    return pl.pallas_call(
        functools.partial(power_kernel, times, chips, total_waves),
        in_specs=[pl.BlockSpec(memory_space=pltpu.VMEM)] * len(operands),
        out_specs=pl.BlockSpec(memory_space=pltpu.VMEM),
        out_shape=jax.ShapeDtypeStruct((peers, rows, LANES), jnp.float32),
        scratch_shapes=[
            pltpu.VMEM((2 * len(chips), waves, low_count, LANES), jnp.bfloat16),
            pltpu.VMEM(basis.shape, jnp.bfloat16),
        ],
        compiler_params=pltpu.CompilerParams(vmem_limit_bytes=24 << 20),
        cost_estimate=pl.CostEstimate(
            flops=16 * waves * held.shape[1] * multipoles * cosmos,
            bytes_accessed=2 * waves * held.shape[1] * multipoles,
            transcendentals=0,
        ),
        name="power",
    )(*operands)


def folds(rows, width):
    spare = LANES - width
    strips = width // spare if spare and width % spare == 0 else 0
    return strips if rows % (8 * (strips + 1)) == 0 else 0


def fold(value):
    rows, width = value.shape
    strips = folds(rows, width)
    if not strips:
        return jnp.concatenate([value, jnp.zeros((rows, LANES - width), value.dtype)], axis=1)
    spare = LANES - width
    head = rows * strips // (strips + 1)
    tail = [value[head:, strip * spare : (strip + 1) * spare] for strip in range(strips)]
    return jnp.concatenate([value[:head], jnp.concatenate(tail, axis=0)], axis=1)


def unfold(value, rows, width):
    strips = folds(rows, width)
    if not strips:
        return value[:, :width]
    size = rows // (strips + 1)
    tail = [value[strip * size : (strip + 1) * size, width:] for strip in range(strips)]
    return jnp.concatenate([value[:, :width], jnp.concatenate(tail, axis=1)], axis=0)


def folded_rows(rows, width):
    strips = folds(rows, width)
    return rows * strips // (strips + 1) if strips else rows


def gradients_kernel(
    parts_ref,
    params_ref,
    coeffs_ref,
    inner_act_ref,
    inner_slope_ref,
    middle_act_ref,
    middle_slope_ref,
    weight_mid_ref,
    weight_out_ref,
    basis_ref,
    offset_ref,
    multipoles_ref,
    spectra_ref,
    grad_basis_ref,
    grad_in_ref,
    grad_mid_ref,
    grad_out_ref,
):
    cosmos = params_ref.shape[1]
    owned, comps = basis_ref.shape
    summed = unfold(jnp.sum(parts_ref[...], axis=0), cosmos, owned + comps)
    spectra = summed[:, :owned] * smoothing_of(multipoles_ref[...])
    coef_grad = summed[:, owned : owned + comps] / cosmos
    coeffs = coeffs_ref[...]
    residual = offset_ref[...] + mat(coeffs, basis_ref[...], ((1,), (1,))) - spectra
    middle_delta = mat(coef_grad, weight_out_ref[...]) * middle_slope_ref[...]
    inner_delta = mat(middle_delta, weight_mid_ref[...]) * inner_slope_ref[...]
    rows = ((0,), (0,))
    spectra_ref[...] = spectra.T
    grad_basis_ref[...] = mat(residual, coeffs, rows) / cosmos
    grad_out_ref[...] = mat(coef_grad, middle_act_ref[...], rows)
    grad_mid_ref[...] = mat(middle_delta, inner_act_ref[...], rows)
    grad_in_ref[...] = mat(params_ref[...], inner_delta)


def gradients(parts, params, coeffs, hidden, weight_mid, weight_out, basis, offset, multipoles):
    count, cosmos = params.shape
    owned, comps = basis.shape
    width = weight_mid.shape[0]
    shape = lambda *dims: jax.ShapeDtypeStruct(dims, jnp.float32)
    return pl.pallas_call(
        gradients_kernel,
        out_shape=(
            shape(owned, cosmos),
            shape(owned, comps),
            shape(count, width),
            shape(width, width),
            shape(comps, width),
        ),
        compiler_params=pltpu.CompilerParams(vmem_limit_bytes=48 << 20),
        name="gradients",
    )(
        parts,
        params,
        coeffs,
        *hidden,
        weight_mid,
        weight_out,
        basis,
        offset.reshape(1, owned),
        multipoles,
    )


def exchange(value, apart, peers):
    return lax.ppermute(value, "ka", [(peer, peer ^ apart) for peer in range(peers)])


def after(value, *others):
    return lax.optimization_barrier((value, *others))[0]


def local(
    sources,
    bessel,
    multipoles,
    window_low,
    window_high,
    params,
    weight_in,
    bias_in,
    weight_mid,
    bias_mid,
    weight_out,
    bias_out,
    pca_basis,
    offset,
):
    waves = bessel.shape[0]
    total_waves = sources.shape[1]
    peers = total_waves // waves
    cosmos = params.shape[1]
    owned = multipoles.shape[0]
    group = LANES // waves
    half = group // 2
    times = sources.shape[0]
    extras = -(-owned // (cosmos * times // LANES))
    me = lax.axis_index("ka").astype(jnp.int32).reshape(1)
    own_multipoles = multipoles.reshape(1, owned)
    turned = jnp.transpose(sources, (0, 2, 1))

    chips = [top * half + low for top in TOPS for low in range(half)]
    late, last = chips[-half:], chips[-1]
    arranged = (turned, own_multipoles, pca_basis, bessel)
    ready = arrange(*arranged, TOPS[:FIRST], group, last)
    *rest_ready, give = arrange(*arranged, TOPS[FIRST:], group, last, HELD)
    held, rest_ready = dict(zip(HELD, rest_ready)), rest_ready[len(HELD) :]
    ready = dict(zip(chips, [*ready, *rest_ready]))
    given = exchange(give, 1, peers)
    got = {}
    near = [chip for chip in chips if 0 < chip < half]
    for chip in chips:
        if chip in (0, last):
            continue
        value = ready[chip]
        if chip in near:
            value = after(value, got[half + near.index(chip)])
        got[chip] = exchange(value, 2 * chip, peers)
    mine, other = ready[last], given[1]
    value = jnp.concatenate([mine[:waves], other[:waves], mine[waves:], other[waves:]])
    got[last] = exchange(value, 2 * last, peers)

    others = lambda part, *then: jnp.stack([after(got[chip], *then)[waves:] for chip in part])
    early = [chip for chip in chips[:-half] if chip]
    traded = exchange(others(early), 1, peers)
    arrays = [traded, given, ready[0]] + [got[chip] for chip in early]
    members = []
    for chip in chips[:-half]:
        if chip:
            at = early.index(chip)
            members += [(2 * chip, 3 + at, None, 0, 2 * waves), (2 * chip + 1, 0, at, 0, waves)]
        else:
            members += [(0, 2, None, 0, waves), (1, 1, 0, 0, waves)]
    rest, basis = add_groups(me, group, arrays, members, bessel, times, extras)
    late_traded = exchange(others(late[:-1], rest), 1, peers)

    inner_pre = mat(params.T, weight_in.T) + bias_in[None, :]
    inner_act = jax.nn.silu(inner_pre)
    middle_pre = mat(inner_act, weight_mid.T) + bias_mid[None, :]
    middle_act = jax.nn.silu(middle_pre)
    coeffs = mat(middle_act, weight_out.T) + bias_out[None, :]
    hidden = (inner_act, silu_slope(inner_pre), middle_act, silu_slope(middle_pre))
    base = mat(offset[None, :] + mat(coeffs, pca_basis.T), pca_basis)

    extra = (params, window_low.reshape(1, cosmos), window_high.reshape(1, cosmos), basis, base)
    pieces = [got[chip] for chip in late]
    parts = power_parts(pieces, late_traded, held[TOPS[-1]], rest, times, late, total_waves, extra)
    gathered = lax.all_to_all(parts, "ka", split_axis=0, concat_axis=0, tiled=True)
    spectra, grad_basis, grad_in, grad_mid, grad_out = gradients(
        gathered, params, coeffs, hidden, weight_mid, weight_out, pca_basis, offset, own_multipoles
    )
    return (spectra, grad_basis, grad_in.T, grad_mid, grad_out)


def solution(mesh):
    return jax.shard_map(
        local,
        mesh=mesh,
        in_specs=(
            P("ka", None, "grp"),
            P("ka", None, None),
            P("ka"),
            P("grp"),
            P("grp"),
            P(None, "grp"),
            P(),
            P(),
            P(),
            P(),
            P(),
            P(),
            P("ka", None),
            P("ka"),
        ),
        out_specs=(
            P("ka", "grp"),
            P(("grp", "ka"), None),
            P("grp", None),
            P("grp", None),
            P("grp", None),
        ),
        check_vma=False,
    )
```

```python
import functools
import math

import jax
import jax.numpy as jnp
from jax import lax
from jax.experimental import pallas as pl
from jax.experimental.pallas import tpu as pltpu
from jax.sharding import PartitionSpec as P

LMAX = 5000
LANES = 128
TOPS = (2, 1, 0, 3)
HELD = (3,)
FIRST = 2
HIGHEST = lax.Precision.HIGHEST


def silu_slope(value):
    sigma = jax.nn.sigmoid(value)
    return sigma * (1.0 + value * (1.0 - sigma))


def mat(left, right, dims=((1,), (0,))):
    return lax.dot_general(
        left, right, (dims, ((), ())), precision=HIGHEST, preferred_element_type=jnp.float32
    )


def split_two(value):
    high = value.astype(jnp.bfloat16)
    low = (value - high.astype(jnp.float32)).astype(jnp.bfloat16)
    return high, low


def smoothing_of(multipoles):
    degree = multipoles.astype(jnp.float32)
    return jnp.exp(-2.0 * degree * (degree + 1.0) / (LMAX * (LMAX + 1.0)))


def column(row):
    return jnp.broadcast_to(row.astype(jnp.float32), (8, row.shape[1])).T[:, :1]


def smooth_basis(multipoles_ref, basis_ref, low_count):
    value = column(smoothing_of(multipoles_ref[...])) * basis_ref[...]
    value = jnp.concatenate([part.astype(jnp.float32) for part in split_two(value)], axis=1)
    spare = -value.shape[0] % low_count
    if spare:
        value = jnp.concatenate([value, jnp.zeros((spare, LANES), jnp.float32)], axis=0)
    return value.astype(jnp.bfloat16).reshape(-1, low_count, LANES)


def arrange_kernel(tops, group, last, waves, held_tops, source_ref, *refs):
    multipoles_ref, basis_ref, whole_ref, *refs = refs
    held_refs, refs = refs[: len(held_tops)], refs[len(held_tops) :]
    *out_refs, block_ref, rows_ref, turned_ref, sems, held_sems = refs
    _, times, cosmos, block = block_ref.shape
    packs = LANES // times
    low_count = cosmos // packs
    size = waves * low_count
    me = lax.axis_index("ka")
    copies = []
    for slot, top in enumerate(tops):
        start = pl.multiple_of(((me // group) ^ top) * block, block)
        copy = pltpu.make_async_copy(
            source_ref.at[:, :, pl.ds(start, block)], block_ref.at[slot], sems.at[slot]
        )
        copy.start()
        copies.append(copy)
    holds = []
    for slot, (top, held_ref) in enumerate(zip(held_tops, held_refs)):
        span = group * times
        start = pl.multiple_of(((me // group) ^ top) * span, span)
        copy = pltpu.make_async_copy(
            whole_ref.at[:, pl.ds(start, span), :], held_ref, held_sems.at[slot]
        )
        copy.start()
        holds.append(copy)
    extra = smooth_basis(multipoles_ref, basis_ref, low_count)
    chips = [top * group // 2 + low for top in tops for low in range(group // 2)]
    for slot, copy in enumerate(copies):
        copy.wait()
        rows_ref[...] = block_ref[slot].astype(jnp.float32).reshape(times * cosmos, block)
        for low in range(low_count):
            pieces = [
                rows_ref[pl.ds(high * low_count + low, times, stride=cosmos), :]
                for high in range(packs)
            ]
            turned_ref[pl.ds(low, block, stride=low_count), :] = jnp.concatenate(pieces, axis=0).T
        for peer in range(group):
            start = pl.multiple_of((peer ^ (me % group)) * size, size)
            piece = turned_ref[pl.ds(start, size), :].astype(jnp.bfloat16)
            piece = piece.reshape(waves, low_count, LANES)
            chip, core = tops[slot] * group // 2 + peer // 2, peer % 2
            out_ref = out_refs[chips.index(chip)]
            if chip in (0, last):
                out_ref = out_refs[-1].at[int(chip == last)] if core else out_ref
                out_ref[:waves] = piece
                out_ref[waves:] = extra
            else:
                out_ref[core * waves : (core + 1) * waves] = piece
                out_ref[2 * waves :] = extra
    for copy in holds:
        copy.wait()


def arrange(sources, multipoles, basis, bessel, tops, group, last, held_tops=()):
    times, cosmos, total = sources.shape
    waves, _, multipole_count = bessel.shape
    low_count = cosmos // (LANES // times)
    block = waves * group
    extras = -(-basis.shape[0] // low_count)
    one, two = (count * waves + extras for count in (1, 2))
    chips = [top * group // 2 + low for top in tops for low in range(group // 2)]
    shapes = [(one if chip in (0, last) else two, low_count, LANES) for chip in chips]
    if last in chips:
        shapes.append((2, one, low_count, LANES))
    held = pltpu.VMEM((waves, group * times, multipole_count), bessel.dtype)
    vmem, anywhere = (pl.BlockSpec(memory_space=space) for space in (pltpu.VMEM, pl.ANY))
    return pl.pallas_call(
        functools.partial(arrange_kernel, tops, group, last, waves, held_tops),
        in_specs=[anywhere, vmem, vmem, anywhere],
        out_specs=[vmem] * (len(held_tops) + len(shapes)),
        out_shape=[held] * len(held_tops)
        + [jax.ShapeDtypeStruct(shape, jnp.bfloat16) for shape in shapes],
        scratch_shapes=[
            pltpu.VMEM((len(tops), times, cosmos, block), jnp.bfloat16),
            pltpu.VMEM((times * cosmos, block), jnp.float32),
            pltpu.VMEM((block * low_count, LANES), jnp.float32),
            pltpu.SemaphoreType.DMA((len(tops),)),
            pltpu.SemaphoreType.DMA((max(1, len(held_tops)),)),
        ],
        compiler_params=pltpu.CompilerParams(vmem_limit_bytes=(50 if held_tops else 61) << 20),
        cost_estimate=pl.CostEstimate(
            flops=0, bytes_accessed=16 * times * cosmos * block * len(tops), transcendentals=0
        ),
        name="arrange",
    )(sources, multipoles, basis, bessel)


def source_rows(stage_ref, wave, times):
    tiles = [stage_ref[peer, wave] for peer in range(stage_ref.shape[0])]
    rows = [
        jnp.concatenate([tile[:, start : start + times] for tile in tiles], axis=1)
        for start in range(0, LANES, times)
    ]
    return jnp.concatenate(rows, axis=0)


def transfer_kernel(group, members, times, me_ref, *refs):
    count = 1 + max(member[1] for member in members)
    arrays, (*bessel_refs, out_ref, basis_ref, stage_ref) = refs[:count], refs[count:]
    me = me_ref[0]
    step = pl.program_id(0)
    waves = out_ref.shape[0]
    extras = basis_ref.shape[1] // stage_ref.shape[3]

    def tiles(array, lead, rows):
        return arrays[array][rows] if lead is None else arrays[array][lead, rows]

    @pl.when(step == 0)
    def _():
        for apart, array, lead, _, at in members:
            extra = tiles(array, lead, pl.ds(at, extras))
            basis_ref[apart] = extra.reshape(basis_ref.shape[1:])

    for number, (_, array, lead, at, _) in enumerate(members):
        place = (number % group) ^ (me % group)
        stage_ref[number // group, place] = tiles(array, lead, pl.ds(at + step * waves, waves))
    for wave in range(waves):
        total = None
        for number, bessel_ref in enumerate(bessel_refs):
            part = jnp.dot(
                source_rows(stage_ref.at[number], wave, times),
                bessel_ref[wave],
                preferred_element_type=jnp.float32,
            )
            total = part if total is None else total + part
        out_ref[wave] = total


def add_groups(me, group, arrays, members, bessel, times, extras):
    low_count = arrays[0].shape[-2]
    waves, _, multipoles = bessel.shape
    span = group * times
    cosmos = low_count * (LANES // times)
    block = math.gcd(waves, 8)
    in_specs = [pl.BlockSpec(memory_space=pltpu.VMEM)] * len(arrays)
    in_specs += [
        pl.BlockSpec(
            (block, span, multipoles), lambda s, me, top=top: (s, (me[0] // group) ^ top, 0)
        )
        for top in TOPS[:-1]
    ]
    basis = (len(members) + group, extras * low_count, LANES)
    return pl.pallas_call(
        functools.partial(transfer_kernel, group, members, times),
        grid_spec=pltpu.PrefetchScalarGridSpec(
            num_scalar_prefetch=1,
            grid=(waves // block,),
            in_specs=in_specs,
            out_specs=[
                pl.BlockSpec((block, cosmos, multipoles), lambda s, me: (s, 0, 0)),
                pl.BlockSpec(basis, lambda s, me: (0, 0, 0)),
            ],
            scratch_shapes=[
                pltpu.VMEM((len(TOPS) - 1, group, block, low_count, LANES), jnp.bfloat16),
            ],
        ),
        out_shape=[
            jax.ShapeDtypeStruct((waves, cosmos, multipoles), jnp.float32),
            jax.ShapeDtypeStruct(basis, jnp.bfloat16),
        ],
        compiler_params=pltpu.CompilerParams(vmem_limit_bytes=24 << 20),
        cost_estimate=pl.CostEstimate(
            flops=16 * math.prod(bessel.shape) * cosmos,
            bytes_accessed=2 * math.prod(bessel.shape),
            transcendentals=0,
        ),
        name="transfer",
    )(me, *arrays, *[bessel] * (len(TOPS) - 1))


def power_kernel(times, chips, total_waves, *refs):
    piece_refs, traded_ref, held_ref, rest_ref, *refs = refs[: len(chips)], *refs[len(chips) :]
    params_ref, low_ref, high_ref, basis_ref, base_ref, out_ref, stage_ref, all_ref = refs
    waves, cosmos, multipoles = rest_ref.shape
    comps = base_ref.shape[1]
    peers = all_ref.shape[0]
    owned = multipoles // peers
    group = 2 * len(chips)
    extras = traded_ref.shape[1] - waves
    me = lax.axis_index("ka")
    all_ref[...] = basis_ref[...]
    for low, (chip, piece_ref) in enumerate(zip(chips, piece_refs)):
        joined = low == len(chips) - 1
        for core in range(2):
            if core and not joined:
                piece, extra = traded_ref[low, :waves], traded_ref[low, waves:]
            else:
                start = 2 * waves + core * extras
                piece, extra = piece_ref[core * waves : (core + 1) * waves], piece_ref[start : start + extras]
            stage_ref[(2 * low + core) ^ (me % group)] = piece
            all_ref[2 * chip + core] = extra.reshape(all_ref.shape[1:])
    first_param, second_param = column(params_ref[0:1]), column(params_ref[1:2])
    low, high = column(low_ref[...]), column(high_ref[...])
    total = jnp.zeros((cosmos, multipoles), jnp.float32)
    for wave in range(waves):
        transfer = rest_ref[wave] + jnp.dot(
            source_rows(stage_ref, wave, times),
            held_ref[wave],
            preferred_element_type=jnp.float32,
        )
        index = (me * waves + wave).astype(jnp.float32)
        log_ratio = math.log(0.002) + index * (math.log(5000.0) / total_waves)
        tilted = 0.5 * first_param + 0.3 * second_param * log_ratio
        inside = (index >= low) & (index < high)
        factor = jnp.where(inside, jnp.exp(tilted), jnp.zeros_like(tilted)) / total_waves
        total = total + transfer * transfer * factor

    basis = jnp.concatenate([all_ref[peer ^ me][:owned] for peer in range(peers)], axis=0)
    power_high, power_low = split_two(total)
    basis_high, basis_low = basis[:, :comps], basis[:, comps:]
    part = base_ref[...]
    for left, right in (
        (power_low, basis_high),
        (power_high, basis_low),
        (power_high, basis_high),
    ):
        part = part - jnp.dot(left, right, preferred_element_type=jnp.float32)
    for peer in range(peers):
        own = total[:, peer * owned : (peer + 1) * owned]
        out_ref[peer] = fold(jnp.concatenate([own, part], axis=1))


def power_parts(pieces, traded, held, rest, times, chips, total_waves, extra):
    low_count = traded.shape[2]
    waves, cosmos, multipoles = rest.shape
    basis, base = extra[-2:]
    peers = basis.shape[0]
    operands = [*pieces, traded, held, rest, *extra]
    rows = folded_rows(cosmos, multipoles // peers + base.shape[1])
    return pl.pallas_call(
        functools.partial(power_kernel, times, chips, total_waves),
        in_specs=[pl.BlockSpec(memory_space=pltpu.VMEM)] * len(operands),
        out_specs=pl.BlockSpec(memory_space=pltpu.VMEM),
        out_shape=jax.ShapeDtypeStruct((peers, rows, LANES), jnp.float32),
        scratch_shapes=[
            pltpu.VMEM((2 * len(chips), waves, low_count, LANES), jnp.bfloat16),
            pltpu.VMEM(basis.shape, jnp.bfloat16),
        ],
        compiler_params=pltpu.CompilerParams(vmem_limit_bytes=24 << 20),
        cost_estimate=pl.CostEstimate(
            flops=16 * waves * held.shape[1] * multipoles * cosmos,
            bytes_accessed=2 * waves * held.shape[1] * multipoles,
            transcendentals=0,
        ),
        name="power",
    )(*operands)


def folds(rows, width):
    spare = LANES - width
    strips = width // spare if spare and width % spare == 0 else 0
    return strips if rows % (8 * (strips + 1)) == 0 else 0


def fold(value):
    rows, width = value.shape
    strips = folds(rows, width)
    if not strips:
        return jnp.concatenate([value, jnp.zeros((rows, LANES - width), value.dtype)], axis=1)
    spare = LANES - width
    head = rows * strips // (strips + 1)
    tail = [value[head:, strip * spare : (strip + 1) * spare] for strip in range(strips)]
    return jnp.concatenate([value[:head], jnp.concatenate(tail, axis=0)], axis=1)


def unfold(value, rows, width):
    strips = folds(rows, width)
    if not strips:
        return value[:, :width]
    size = rows // (strips + 1)
    tail = [value[strip * size : (strip + 1) * size, width:] for strip in range(strips)]
    return jnp.concatenate([value[:, :width], jnp.concatenate(tail, axis=1)], axis=0)


def folded_rows(rows, width):
    strips = folds(rows, width)
    return rows * strips // (strips + 1) if strips else rows


def near_mat(left, right, dims=((1,), (0,))):
    left_high, left_low = split_two(left)
    right_high, right_low = split_two(right)
    parts = ((left_low, right_high), (left_high, right_low), (left_high, right_high))
    return sum(
        lax.dot_general(one, other, (dims, ((), ())), preferred_element_type=jnp.float32)
        for one, other in parts
    )


def gradients_kernel(
    parts_ref,
    params_ref,
    coeffs_ref,
    inner_act_ref,
    inner_slope_ref,
    middle_act_ref,
    middle_slope_ref,
    weight_mid_ref,
    weight_out_ref,
    basis_ref,
    offset_ref,
    multipoles_ref,
    *refs,
):
    out_refs, (*value_refs, sems) = refs[:5], refs[5:]
    cosmos = params_ref.shape[1]
    owned, comps = basis_ref.shape
    copies = []

    def store(number, value):
        value_refs[number][...] = value
        copy = pltpu.make_async_copy(value_refs[number], out_refs[number], sems.at[number])
        copy.start()
        copies.append(copy)

    rows = ((0,), (0,))
    summed = unfold(jnp.sum(parts_ref[...], axis=0), cosmos, owned + comps)
    coef_grad = summed[:, owned : owned + comps] / cosmos
    middle_delta = near_mat(coef_grad, weight_out_ref[...]) * middle_slope_ref[...]
    store(3, near_mat(middle_delta, inner_act_ref[...], rows))
    inner_delta = near_mat(middle_delta, weight_mid_ref[...]) * inner_slope_ref[...]
    store(4, near_mat(coef_grad, middle_act_ref[...], rows))
    spectra = summed[:, :owned] * smoothing_of(multipoles_ref[...])
    coeffs = coeffs_ref[...]
    residual = offset_ref[...] + near_mat(coeffs, basis_ref[...], ((1,), (1,))) - spectra
    store(0, spectra.T)
    store(1, near_mat(residual, coeffs, rows) / cosmos)
    store(2, near_mat(params_ref[...], inner_delta))
    for copy in copies:
        copy.wait()


def gradients(parts, params, coeffs, hidden, weight_mid, weight_out, basis, offset, multipoles):
    count, cosmos = params.shape
    owned, comps = basis.shape
    width = weight_mid.shape[0]
    shapes = ((owned, cosmos), (owned, comps), (count, width), (width, width), (comps, width))
    operands = (parts, params, coeffs, *hidden, weight_mid, weight_out, basis)
    operands += (offset.reshape(1, owned), multipoles)
    return pl.pallas_call(
        gradients_kernel,
        in_specs=[pl.BlockSpec(memory_space=pltpu.VMEM)] * len(operands),
        out_specs=[pl.BlockSpec(memory_space=pl.ANY)] * len(shapes),
        out_shape=[jax.ShapeDtypeStruct(shape, jnp.float32) for shape in shapes],
        scratch_shapes=[pltpu.VMEM(shape, jnp.float32) for shape in shapes]
        + [pltpu.SemaphoreType.DMA((len(shapes),))],
        compiler_params=pltpu.CompilerParams(vmem_limit_bytes=24 << 20),
        name="gradients",
    )(*operands)


def exchange(value, apart, peers):
    return lax.ppermute(value, "ka", [(peer, peer ^ apart) for peer in range(peers)])


def after(value, *others):
    return lax.optimization_barrier((value, *others))[0]


def local(
    sources,
    bessel,
    multipoles,
    window_low,
    window_high,
    params,
    weight_in,
    bias_in,
    weight_mid,
    bias_mid,
    weight_out,
    bias_out,
    pca_basis,
    offset,
):
    waves = bessel.shape[0]
    total_waves = sources.shape[1]
    peers = total_waves // waves
    cosmos = params.shape[1]
    owned = multipoles.shape[0]
    group = LANES // waves
    half = group // 2
    times = sources.shape[0]
    extras = -(-owned // (cosmos * times // LANES))
    me = lax.axis_index("ka").astype(jnp.int32).reshape(1)
    own_multipoles = multipoles.reshape(1, owned)
    turned = jnp.transpose(sources, (0, 2, 1))

    chips = [top * half + low for top in TOPS for low in range(half)]
    late, last = chips[-half:], chips[-1]
    arranged = (turned, own_multipoles, pca_basis, bessel)
    ready = arrange(*arranged, TOPS[:FIRST], group, last)
    *rest_ready, give = arrange(*arranged, TOPS[FIRST:], group, last, HELD)
    held, rest_ready = dict(zip(HELD, rest_ready)), rest_ready[len(HELD) :]
    ready = dict(zip(chips, [*ready, *rest_ready]))
    got = {}
    near = [chip for chip in chips if 0 < chip < half]
    for chip in chips:
        if chip in (0, last):
            continue
        value = ready[chip]
        if chip in near:
            value = after(value, got[TOPS[0] * half])
        got[chip] = exchange(value, 2 * chip, peers)
    given = exchange(after(give, got[TOPS[0] * half]), 1, peers)
    mine, other = ready[last], given[1]
    value = jnp.concatenate([mine[:waves], other[:waves], mine[waves:], other[waves:]])
    got[last] = exchange(value, 2 * last, peers)

    others = lambda part, *then: jnp.stack([after(got[chip], *then)[waves:] for chip in part])
    early = [chip for chip in chips[:-half] if chip]
    traded = exchange(others(early), 1, peers)
    arrays = [traded, given, ready[0]] + [got[chip] for chip in early]
    members = []
    for chip in chips[:-half]:
        if chip:
            at = early.index(chip)
            members += [(2 * chip, 3 + at, None, 0, 2 * waves), (2 * chip + 1, 0, at, 0, waves)]
        else:
            members += [(0, 2, None, 0, waves), (1, 1, 0, 0, waves)]
    rest, basis = add_groups(me, group, arrays, members, bessel, times, extras)
    late_traded = exchange(others(late[:-1], rest), 1, peers)

    inner_pre = mat(params.T, weight_in.T) + bias_in[None, :]
    inner_act = jax.nn.silu(inner_pre)
    middle_pre = mat(inner_act, weight_mid.T) + bias_mid[None, :]
    middle_act = jax.nn.silu(middle_pre)
    coeffs = mat(middle_act, weight_out.T) + bias_out[None, :]
    hidden = (inner_act, silu_slope(inner_pre), middle_act, silu_slope(middle_pre))
    base = mat(offset[None, :] + mat(coeffs, pca_basis.T), pca_basis)

    extra = (params, window_low.reshape(1, cosmos), window_high.reshape(1, cosmos), basis, base)
    pieces = [got[chip] for chip in late]
    parts = power_parts(pieces, late_traded, held[TOPS[-1]], rest, times, late, total_waves, extra)
    gathered = lax.all_to_all(parts, "ka", split_axis=0, concat_axis=0, tiled=True)
    spectra, grad_basis, grad_in, grad_mid, grad_out = gradients(
        gathered, params, coeffs, hidden, weight_mid, weight_out, pca_basis, offset, own_multipoles
    )
    return (spectra, grad_basis, grad_in.T, grad_mid, grad_out)


def solution(mesh):
    return jax.shard_map(
        local,
        mesh=mesh,
        in_specs=(
            P("ka", None, "grp"),
            P("ka", None, None),
            P("ka"),
            P("grp"),
            P("grp"),
            P(None, "grp"),
            P(),
            P(),
            P(),
            P(),
            P(),
            P(),
            P("ka", None),
            P("ka"),
        ),
        out_specs=(
            P("ka", "grp"),
            P(("grp", "ka"), None),
            P("grp", None),
            P("grp", None),
            P("grp", None),
        ),
        check_vma=False,
    )
```

```python
import functools
import math

import jax
import jax.numpy as jnp
from jax import lax
from jax.experimental import pallas as pl
from jax.experimental.pallas import tpu as pltpu
from jax.sharding import PartitionSpec as P

LMAX = 5000
LANES = 128
TOPS = (2, 1, 0, 3)
HELD = (3,)
FIRST = 2
HIGHEST = lax.Precision.HIGHEST


def silu_slope(value):
    sigma = jax.nn.sigmoid(value)
    return sigma * (1.0 + value * (1.0 - sigma))


def mat(left, right, dims=((1,), (0,))):
    return lax.dot_general(
        left, right, (dims, ((), ())), precision=HIGHEST, preferred_element_type=jnp.float32
    )


def split_two(value):
    high = value.astype(jnp.bfloat16)
    low = (value - high.astype(jnp.float32)).astype(jnp.bfloat16)
    return high, low


def smoothing_of(multipoles):
    degree = multipoles.astype(jnp.float32)
    return jnp.exp(-2.0 * degree * (degree + 1.0) / (LMAX * (LMAX + 1.0)))


def column(row):
    return jnp.broadcast_to(row.astype(jnp.float32), (8, row.shape[1])).T[:, :1]


def smooth_basis(multipoles_ref, basis_ref, low_count):
    value = column(smoothing_of(multipoles_ref[...])) * basis_ref[...]
    value = jnp.concatenate([part.astype(jnp.float32) for part in split_two(value)], axis=1)
    spare = -value.shape[0] % low_count
    if spare:
        value = jnp.concatenate([value, jnp.zeros((spare, LANES), jnp.float32)], axis=0)
    return value.astype(jnp.bfloat16).reshape(-1, low_count, LANES)


def arrange_kernel(tops, group, last, waves, held_tops, source_ref, *refs):
    multipoles_ref, basis_ref, whole_ref, *refs = refs
    held_refs, refs = refs[: len(held_tops)], refs[len(held_tops) :]
    *out_refs, block_ref, rows_ref, turned_ref, sems, held_sems = refs
    _, times, cosmos, block = block_ref.shape
    packs = LANES // times
    low_count = cosmos // packs
    size = waves * low_count
    me = lax.axis_index("ka")
    copies = []
    for slot, top in enumerate(tops):
        start = pl.multiple_of(((me // group) ^ top) * block, block)
        copy = pltpu.make_async_copy(
            source_ref.at[:, :, pl.ds(start, block)], block_ref.at[slot], sems.at[slot]
        )
        copy.start()
        copies.append(copy)
    holds = []
    for slot, (top, held_ref) in enumerate(zip(held_tops, held_refs)):
        span = group * times
        start = pl.multiple_of(((me // group) ^ top) * span, span)
        copy = pltpu.make_async_copy(
            whole_ref.at[:, pl.ds(start, span), :], held_ref, held_sems.at[slot]
        )
        copy.start()
        holds.append(copy)
    extra = smooth_basis(multipoles_ref, basis_ref, low_count)
    chips = [top * group // 2 + low for top in tops for low in range(group // 2)]
    for slot, copy in enumerate(copies):
        copy.wait()
        rows = block_ref[slot].astype(jnp.float32).reshape(times * cosmos, block)
        rows_ref[: times * cosmos] = rows
        for low in range(low_count):
            pieces = [
                rows_ref[pl.ds(high * low_count + low, times, stride=cosmos), :]
                for high in range(packs)
            ]
            turned_ref[pl.ds(low, block, stride=low_count), :] = jnp.concatenate(pieces, axis=0).T
        for peer in range(group):
            start = pl.multiple_of((peer ^ (me % group)) * size, size)
            piece = turned_ref[pl.ds(start, size), :].astype(jnp.bfloat16)
            piece = piece.reshape(waves, low_count, LANES)
            chip, core = tops[slot] * group // 2 + peer // 2, peer % 2
            out_ref = out_refs[chips.index(chip)]
            if chip in (0, last):
                out_ref = out_refs[-1].at[int(chip == last)] if core else out_ref
                out_ref[:waves] = piece
                out_ref[waves:] = extra
            else:
                out_ref[core * waves : (core + 1) * waves] = piece
                out_ref[2 * waves :] = extra
    for copy in holds:
        copy.wait()


def arrange(sources, multipoles, basis, bessel, tops, group, last, held_tops=()):
    times, cosmos, total = sources.shape
    waves, _, multipole_count = bessel.shape
    low_count = cosmos // (LANES // times)
    block = waves * group
    extras = -(-basis.shape[0] // low_count)
    one, two = (count * waves + extras for count in (1, 2))
    chips = [top * group // 2 + low for top in tops for low in range(group // 2)]
    shapes = [(one if chip in (0, last) else two, low_count, LANES) for chip in chips]
    if last in chips:
        shapes.append((2, one, low_count, LANES))
    held = pltpu.VMEM((waves, group * times, multipole_count), bessel.dtype)
    vmem, anywhere = (pl.BlockSpec(memory_space=space) for space in (pltpu.VMEM, pl.ANY))
    return pl.pallas_call(
        functools.partial(arrange_kernel, tops, group, last, waves, held_tops),
        in_specs=[anywhere, vmem, vmem, anywhere],
        out_specs=[vmem] * (len(held_tops) + len(shapes)),
        out_shape=[held] * len(held_tops)
        + [jax.ShapeDtypeStruct(shape, jnp.bfloat16) for shape in shapes],
        scratch_shapes=[
            pltpu.VMEM((len(tops), times, cosmos, block), jnp.bfloat16),
            pltpu.VMEM(((times + 1) * cosmos, block), jnp.float32),
            pltpu.VMEM(((block + 1) * low_count, LANES), jnp.float32),
            pltpu.SemaphoreType.DMA((len(tops),)),
            pltpu.SemaphoreType.DMA((max(1, len(held_tops)),)),
        ],
        compiler_params=pltpu.CompilerParams(vmem_limit_bytes=(50 if held_tops else 61) << 20),
        cost_estimate=pl.CostEstimate(
            flops=0, bytes_accessed=16 * times * cosmos * block * len(tops), transcendentals=0
        ),
        name="arrange",
    )(sources, multipoles, basis, bessel)


def source_rows(stage_ref, wave, times):
    tiles = [stage_ref[peer, wave] for peer in range(stage_ref.shape[0])]
    rows = [
        jnp.concatenate([tile[:, start : start + times] for tile in tiles], axis=1)
        for start in range(0, LANES, times)
    ]
    return jnp.concatenate(rows, axis=0)


def transfer_kernel(group, members, times, me_ref, *refs):
    count = 1 + max(member[1] for member in members)
    arrays, (*bessel_refs, out_ref, basis_ref, stage_ref) = refs[:count], refs[count:]
    me = me_ref[0]
    step = pl.program_id(0)
    waves = out_ref.shape[0]
    extras = basis_ref.shape[1] // stage_ref.shape[3]

    def tiles(array, lead, rows):
        return arrays[array][rows] if lead is None else arrays[array][lead, rows]

    @pl.when(step == 0)
    def _():
        for apart, array, lead, _, at in members:
            extra = tiles(array, lead, pl.ds(at, extras))
            basis_ref[apart] = extra.reshape(basis_ref.shape[1:])

    for number, (_, array, lead, at, _) in enumerate(members):
        place = (number % group) ^ (me % group)
        stage_ref[number // group, place] = tiles(array, lead, pl.ds(at + step * waves, waves))
    for wave in range(waves):
        total = None
        for number, bessel_ref in enumerate(bessel_refs):
            part = jnp.dot(
                source_rows(stage_ref.at[number], wave, times),
                bessel_ref[wave],
                preferred_element_type=jnp.float32,
            )
            total = part if total is None else total + part
        out_ref[wave] = total


def add_groups(me, group, arrays, members, bessel, times, extras):
    low_count = arrays[0].shape[-2]
    waves, _, multipoles = bessel.shape
    span = group * times
    cosmos = low_count * (LANES // times)
    block = math.gcd(waves, 8)
    in_specs = [pl.BlockSpec(memory_space=pltpu.VMEM)] * len(arrays)
    in_specs += [
        pl.BlockSpec(
            (block, span, multipoles), lambda s, me, top=top: (s, (me[0] // group) ^ top, 0)
        )
        for top in TOPS[:-1]
    ]
    basis = (len(members) + group, extras * low_count, LANES)
    return pl.pallas_call(
        functools.partial(transfer_kernel, group, members, times),
        grid_spec=pltpu.PrefetchScalarGridSpec(
            num_scalar_prefetch=1,
            grid=(waves // block,),
            in_specs=in_specs,
            out_specs=[
                pl.BlockSpec((block, cosmos, multipoles), lambda s, me: (s, 0, 0)),
                pl.BlockSpec(basis, lambda s, me: (0, 0, 0)),
            ],
            scratch_shapes=[
                pltpu.VMEM((len(TOPS) - 1, group, block, low_count, LANES), jnp.bfloat16),
            ],
        ),
        out_shape=[
            jax.ShapeDtypeStruct((waves, cosmos, multipoles), jnp.float32),
            jax.ShapeDtypeStruct(basis, jnp.bfloat16),
        ],
        compiler_params=pltpu.CompilerParams(vmem_limit_bytes=24 << 20),
        cost_estimate=pl.CostEstimate(
            flops=16 * math.prod(bessel.shape) * cosmos,
            bytes_accessed=2 * math.prod(bessel.shape),
            transcendentals=0,
        ),
        name="transfer",
    )(me, *arrays, *[bessel] * (len(TOPS) - 1))


def power_kernel(times, chips, total_waves, *refs):
    piece_refs, traded_ref, held_ref, rest_ref, *refs = refs[: len(chips)], *refs[len(chips) :]
    params_ref, low_ref, high_ref, basis_ref, base_ref, out_ref, stage_ref, all_ref = refs
    waves, cosmos, multipoles = rest_ref.shape
    comps = base_ref.shape[1]
    peers = all_ref.shape[0]
    owned = multipoles // peers
    group = 2 * len(chips)
    extras = traded_ref.shape[1] - waves
    me = lax.axis_index("ka")
    all_ref[...] = basis_ref[...]
    for low, (chip, piece_ref) in enumerate(zip(chips, piece_refs)):
        joined = low == len(chips) - 1
        for core in range(2):
            if core and not joined:
                piece, extra = traded_ref[low, :waves], traded_ref[low, waves:]
            else:
                start = 2 * waves + core * extras
                piece, extra = piece_ref[core * waves : (core + 1) * waves], piece_ref[start : start + extras]
            stage_ref[(2 * low + core) ^ (me % group)] = piece
            all_ref[2 * chip + core] = extra.reshape(all_ref.shape[1:])
    first_param, second_param = column(params_ref[0:1]), column(params_ref[1:2])
    low, high = column(low_ref[...]), column(high_ref[...])
    total = jnp.zeros((cosmos, multipoles), jnp.float32)
    for wave in range(waves):
        transfer = rest_ref[wave] + jnp.dot(
            source_rows(stage_ref, wave, times),
            held_ref[wave],
            preferred_element_type=jnp.float32,
        )
        index = (me * waves + wave).astype(jnp.float32)
        log_ratio = math.log(0.002) + index * (math.log(5000.0) / total_waves)
        tilted = 0.5 * first_param + 0.3 * second_param * log_ratio
        inside = (index >= low) & (index < high)
        factor = jnp.where(inside, jnp.exp(tilted), jnp.zeros_like(tilted)) / total_waves
        total = total + transfer * transfer * factor

    basis = jnp.concatenate([all_ref[peer ^ me][:owned] for peer in range(peers)], axis=0)
    power_high, power_low = split_two(total)
    basis_high, basis_low = basis[:, :comps], basis[:, comps:]
    part = base_ref[...]
    for left, right in (
        (power_low, basis_high),
        (power_high, basis_low),
        (power_high, basis_high),
    ):
        part = part - jnp.dot(left, right, preferred_element_type=jnp.float32)
    for peer in range(peers):
        own = total[:, peer * owned : (peer + 1) * owned]
        out_ref[peer] = fold(jnp.concatenate([own, part], axis=1))


def power_parts(pieces, traded, held, rest, times, chips, total_waves, extra):
    low_count = traded.shape[2]
    waves, cosmos, multipoles = rest.shape
    basis, base = extra[-2:]
    peers = basis.shape[0]
    operands = [*pieces, traded, held, rest, *extra]
    rows = folded_rows(cosmos, multipoles // peers + base.shape[1])
    return pl.pallas_call(
        functools.partial(power_kernel, times, chips, total_waves),
        in_specs=[pl.BlockSpec(memory_space=pltpu.VMEM)] * len(operands),
        out_specs=pl.BlockSpec(memory_space=pltpu.VMEM),
        out_shape=jax.ShapeDtypeStruct((peers, rows, LANES), jnp.float32),
        scratch_shapes=[
            pltpu.VMEM((2 * len(chips), waves, low_count, LANES), jnp.bfloat16),
            pltpu.VMEM(basis.shape, jnp.bfloat16),
        ],
        compiler_params=pltpu.CompilerParams(vmem_limit_bytes=24 << 20),
        cost_estimate=pl.CostEstimate(
            flops=16 * waves * held.shape[1] * multipoles * cosmos,
            bytes_accessed=2 * waves * held.shape[1] * multipoles,
            transcendentals=0,
        ),
        name="power",
    )(*operands)


def folds(rows, width):
    spare = LANES - width
    strips = width // spare if spare and width % spare == 0 else 0
    return strips if rows % (8 * (strips + 1)) == 0 else 0


def fold(value):
    rows, width = value.shape
    strips = folds(rows, width)
    if not strips:
        return jnp.concatenate([value, jnp.zeros((rows, LANES - width), value.dtype)], axis=1)
    spare = LANES - width
    head = rows * strips // (strips + 1)
    tail = [value[head:, strip * spare : (strip + 1) * spare] for strip in range(strips)]
    return jnp.concatenate([value[:head], jnp.concatenate(tail, axis=0)], axis=1)


def unfold(value, rows, width):
    strips = folds(rows, width)
    if not strips:
        return value[:, :width]
    size = rows // (strips + 1)
    tail = [value[strip * size : (strip + 1) * size, width:] for strip in range(strips)]
    return jnp.concatenate([value[:, :width], jnp.concatenate(tail, axis=1)], axis=0)


def folded_rows(rows, width):
    strips = folds(rows, width)
    return rows * strips // (strips + 1) if strips else rows


def near_mat(left, right, dims=((1,), (0,))):
    left_high, left_low = split_two(left)
    right_high, right_low = split_two(right)
    parts = ((left_low, right_high), (left_high, right_low), (left_high, right_high))
    return sum(
        lax.dot_general(one, other, (dims, ((), ())), preferred_element_type=jnp.float32)
        for one, other in parts
    )


def gradients_kernel(
    parts_ref,
    params_ref,
    coeffs_ref,
    inner_act_ref,
    inner_slope_ref,
    middle_act_ref,
    middle_slope_ref,
    weight_mid_ref,
    weight_out_ref,
    basis_ref,
    offset_ref,
    multipoles_ref,
    *refs,
):
    out_refs, (*value_refs, sems) = refs[:5], refs[5:]
    cosmos = params_ref.shape[1]
    owned, comps = basis_ref.shape
    copies = []

    def store(number, value):
        value_refs[number][...] = value
        copy = pltpu.make_async_copy(value_refs[number], out_refs[number], sems.at[number])
        copy.start()
        copies.append(copy)

    rows = ((0,), (0,))
    summed = unfold(jnp.sum(parts_ref[...], axis=0), cosmos, owned + comps)
    coef_grad = summed[:, owned : owned + comps] / cosmos
    middle_delta = near_mat(coef_grad, weight_out_ref[...]) * middle_slope_ref[...]
    store(3, near_mat(middle_delta, inner_act_ref[...], rows))
    inner_delta = near_mat(middle_delta, weight_mid_ref[...]) * inner_slope_ref[...]
    store(4, near_mat(coef_grad, middle_act_ref[...], rows))
    spectra = summed[:, :owned] * smoothing_of(multipoles_ref[...])
    coeffs = coeffs_ref[...]
    residual = offset_ref[...] + near_mat(coeffs, basis_ref[...], ((1,), (1,))) - spectra
    store(0, spectra.T)
    store(1, near_mat(residual, coeffs, rows) / cosmos)
    store(2, near_mat(params_ref[...], inner_delta))
    for copy in copies:
        copy.wait()


def gradients(parts, params, coeffs, hidden, weight_mid, weight_out, basis, offset, multipoles):
    count, cosmos = params.shape
    owned, comps = basis.shape
    width = weight_mid.shape[0]
    shapes = ((owned, cosmos), (owned, comps), (count, width), (width, width), (comps, width))
    operands = (parts, params, coeffs, *hidden, weight_mid, weight_out, basis)
    operands += (offset.reshape(1, owned), multipoles)
    return pl.pallas_call(
        gradients_kernel,
        in_specs=[pl.BlockSpec(memory_space=pltpu.VMEM)] * len(operands),
        out_specs=[pl.BlockSpec(memory_space=pl.ANY)] * len(shapes),
        out_shape=[jax.ShapeDtypeStruct(shape, jnp.float32) for shape in shapes],
        scratch_shapes=[pltpu.VMEM(shape, jnp.float32) for shape in shapes]
        + [pltpu.SemaphoreType.DMA((len(shapes),))],
        compiler_params=pltpu.CompilerParams(vmem_limit_bytes=24 << 20),
        name="gradients",
    )(*operands)


def exchange(value, apart, peers):
    return lax.ppermute(value, "ka", [(peer, peer ^ apart) for peer in range(peers)])


def after(value, *others):
    return lax.optimization_barrier((value, *others))[0]


def local(
    sources,
    bessel,
    multipoles,
    window_low,
    window_high,
    params,
    weight_in,
    bias_in,
    weight_mid,
    bias_mid,
    weight_out,
    bias_out,
    pca_basis,
    offset,
):
    waves = bessel.shape[0]
    total_waves = sources.shape[1]
    peers = total_waves // waves
    cosmos = params.shape[1]
    owned = multipoles.shape[0]
    group = LANES // waves
    half = group // 2
    times = sources.shape[0]
    extras = -(-owned // (cosmos * times // LANES))
    me = lax.axis_index("ka").astype(jnp.int32).reshape(1)
    own_multipoles = multipoles.reshape(1, owned)
    turned = jnp.transpose(sources, (0, 2, 1))

    chips = [top * half + low for top in TOPS for low in range(half)]
    late, last = chips[-half:], chips[-1]
    arranged = (turned, own_multipoles, pca_basis, bessel)
    ready = arrange(*arranged, TOPS[:FIRST], group, last)
    *rest_ready, give = arrange(*arranged, TOPS[FIRST:], group, last, HELD)
    held, rest_ready = dict(zip(HELD, rest_ready)), rest_ready[len(HELD) :]
    ready = dict(zip(chips, [*ready, *rest_ready]))
    got = {}
    near = [chip for chip in chips if 0 < chip < half]
    for chip in chips:
        if chip in (0, last):
            continue
        value = ready[chip]
        if chip in near:
            value = after(value, got[TOPS[0] * half])
        got[chip] = exchange(value, 2 * chip, peers)
    given = exchange(after(give, got[TOPS[0] * half]), 1, peers)
    mine, other = ready[last], given[1]
    value = jnp.concatenate([mine[:waves], other[:waves], mine[waves:], other[waves:]])
    got[last] = exchange(value, 2 * last, peers)

    others = lambda part, *then: jnp.stack([after(got[chip], *then)[waves:] for chip in part])
    early = [chip for chip in chips[:-half] if chip]
    traded = exchange(others(early), 1, peers)
    arrays = [traded, given, ready[0]] + [got[chip] for chip in early]
    members = []
    for chip in chips[:-half]:
        if chip:
            at = early.index(chip)
            members += [(2 * chip, 3 + at, None, 0, 2 * waves), (2 * chip + 1, 0, at, 0, waves)]
        else:
            members += [(0, 2, None, 0, waves), (1, 1, 0, 0, waves)]
    rest, basis = add_groups(me, group, arrays, members, bessel, times, extras)
    late_traded = exchange(others(late[:-1], rest), 1, peers)

    inner_pre = mat(params.T, weight_in.T) + bias_in[None, :]
    inner_act = jax.nn.silu(inner_pre)
    middle_pre = mat(inner_act, weight_mid.T) + bias_mid[None, :]
    middle_act = jax.nn.silu(middle_pre)
    coeffs = mat(middle_act, weight_out.T) + bias_out[None, :]
    hidden = (inner_act, silu_slope(inner_pre), middle_act, silu_slope(middle_pre))
    base = mat(offset[None, :] + mat(coeffs, pca_basis.T), pca_basis)

    extra = (params, window_low.reshape(1, cosmos), window_high.reshape(1, cosmos), basis, base)
    pieces = [got[chip] for chip in late]
    parts = power_parts(pieces, late_traded, held[TOPS[-1]], rest, times, late, total_waves, extra)
    gathered = lax.all_to_all(parts, "ka", split_axis=0, concat_axis=0, tiled=True)
    spectra, grad_basis, grad_in, grad_mid, grad_out = gradients(
        gathered, params, coeffs, hidden, weight_mid, weight_out, pca_basis, offset, own_multipoles
    )
    return (spectra, grad_basis, grad_in.T, grad_mid, grad_out)


def solution(mesh):
    return jax.shard_map(
        local,
        mesh=mesh,
        in_specs=(
            P("ka", None, "grp"),
            P("ka", None, None),
            P("ka"),
            P("grp"),
            P("grp"),
            P(None, "grp"),
            P(),
            P(),
            P(),
            P(),
            P(),
            P(),
            P("ka", None),
            P("ka"),
        ),
        out_specs=(
            P("ka", "grp"),
            P(("grp", "ka"), None),
            P("grp", None),
            P("grp", None),
            P("grp", None),
        ),
        check_vma=False,
    )
```

```python
import functools
import math

import jax
import jax.numpy as jnp
from jax import lax
from jax.experimental import pallas as pl
from jax.experimental.pallas import tpu as pltpu
from jax.sharding import PartitionSpec as P

LMAX = 5000
LANES = 128
TOPS = (2, 1, 0, 3)
HELD = (3,)
FIRST = 2
HIGHEST = lax.Precision.HIGHEST


def silu_slope(value):
    sigma = jax.nn.sigmoid(value)
    return sigma * (1.0 + value * (1.0 - sigma))


def mat(left, right, dims=((1,), (0,))):
    return lax.dot_general(
        left, right, (dims, ((), ())), precision=HIGHEST, preferred_element_type=jnp.float32
    )


def split_two(value):
    high = value.astype(jnp.bfloat16)
    low = (value - high.astype(jnp.float32)).astype(jnp.bfloat16)
    return high, low


def smoothing_of(multipoles):
    degree = multipoles.astype(jnp.float32)
    return jnp.exp(-2.0 * degree * (degree + 1.0) / (LMAX * (LMAX + 1.0)))


def column(row):
    return jnp.broadcast_to(row.astype(jnp.float32), (8, row.shape[1])).T[:, :1]


def smooth_basis(multipoles_ref, basis_ref, low_count):
    value = column(smoothing_of(multipoles_ref[...])) * basis_ref[...]
    value = jnp.concatenate([part.astype(jnp.float32) for part in split_two(value)], axis=1)
    spare = -value.shape[0] % low_count
    if spare:
        value = jnp.concatenate([value, jnp.zeros((spare, LANES), jnp.float32)], axis=0)
    return value.astype(jnp.bfloat16).reshape(-1, low_count, LANES)


def arrange_kernel(tops, group, last, waves, held_tops, source_ref, *refs):
    multipoles_ref, basis_ref, whole_ref, *refs = refs
    held_refs, refs = refs[: len(held_tops)], refs[len(held_tops) :]
    *out_refs, block_ref, rows_ref, turned_ref, sems, held_sems = refs
    _, times, cosmos, block = block_ref.shape
    packs = LANES // times
    low_count = cosmos // packs
    size = waves * low_count
    me = lax.axis_index("ka")
    copies = []
    for slot, top in enumerate(tops):
        start = pl.multiple_of(((me // group) ^ top) * block, block)
        copy = pltpu.make_async_copy(
            source_ref.at[:, :, pl.ds(start, block)], block_ref.at[slot], sems.at[slot]
        )
        copy.start()
        copies.append(copy)
    holds = []
    for slot, (top, held_ref) in enumerate(zip(held_tops, held_refs)):
        span = group * times
        start = pl.multiple_of(((me // group) ^ top) * span, span)
        copy = pltpu.make_async_copy(
            whole_ref.at[:, pl.ds(start, span), :], held_ref, held_sems.at[slot]
        )
        copy.start()
        holds.append(copy)
    extra = smooth_basis(multipoles_ref, basis_ref, low_count)
    chips = [top * group // 2 + low for top in tops for low in range(group // 2)]
    for slot, copy in enumerate(copies):
        copy.wait()
        rows = block_ref[slot].astype(jnp.float32).reshape(times * cosmos, block)
        rows_ref[: times * cosmos] = rows
        for low in range(low_count):
            pieces = [
                rows_ref[pl.ds(high * low_count + low, times, stride=cosmos), :]
                for high in range(packs)
            ]
            turned_ref[pl.ds(low, block, stride=low_count), :] = jnp.concatenate(pieces, axis=0).T
        for peer in range(group):
            start = pl.multiple_of((peer ^ (me % group)) * size, size)
            piece = turned_ref[pl.ds(start, size), :].astype(jnp.bfloat16)
            piece = piece.reshape(waves, low_count, LANES)
            chip, core = tops[slot] * group // 2 + peer // 2, peer % 2
            out_ref = out_refs[chips.index(chip)]
            if chip in (0, last):
                out_ref = out_refs[-1].at[int(chip == last)] if core else out_ref
                out_ref[:waves] = piece
                if core or chip == 0:
                    out_ref[waves:] = extra
            else:
                out_ref[core * waves : (core + 1) * waves] = piece
                if tops[slot] != TOPS[-1]:
                    out_ref[2 * waves :] = extra
    for copy in holds:
        copy.wait()


def arrange(sources, multipoles, basis, bessel, tops, group, last, held_tops=()):
    times, cosmos, total = sources.shape
    waves, _, multipole_count = bessel.shape
    low_count = cosmos // (LANES // times)
    block = waves * group
    extras = -(-basis.shape[0] // low_count)
    one, two = (count * waves + extras for count in (1, 2))
    chips = [top * group // 2 + low for top in tops for low in range(group // 2)]
    late = range(TOPS[-1] * group // 2, TOPS[-1] * group // 2 + group // 2)
    tiles = [(one if chip in (0, last) else two) - (extras if chip in late else 0) for chip in chips]
    shapes = [(count, low_count, LANES) for count in tiles]
    if last in chips:
        shapes.append((2, one, low_count, LANES))
    held = pltpu.VMEM((waves, group * times, multipole_count), bessel.dtype)
    vmem, anywhere = (pl.BlockSpec(memory_space=space) for space in (pltpu.VMEM, pl.ANY))
    return pl.pallas_call(
        functools.partial(arrange_kernel, tops, group, last, waves, held_tops),
        in_specs=[anywhere, vmem, vmem, anywhere],
        out_specs=[vmem] * (len(held_tops) + len(shapes)),
        out_shape=[held] * len(held_tops)
        + [jax.ShapeDtypeStruct(shape, jnp.bfloat16) for shape in shapes],
        scratch_shapes=[
            pltpu.VMEM((len(tops), times, cosmos, block), jnp.bfloat16),
            pltpu.VMEM(((times + 1) * cosmos, block), jnp.float32),
            pltpu.VMEM(((block + 1) * low_count, LANES), jnp.float32),
            pltpu.SemaphoreType.DMA((len(tops),)),
            pltpu.SemaphoreType.DMA((max(1, len(held_tops)),)),
        ],
        compiler_params=pltpu.CompilerParams(vmem_limit_bytes=(50 if held_tops else 61) << 20),
        cost_estimate=pl.CostEstimate(
            flops=0, bytes_accessed=16 * times * cosmos * block * len(tops), transcendentals=0
        ),
        name="arrange",
    )(sources, multipoles, basis, bessel)


def source_rows(stage_ref, wave, times):
    tiles = [stage_ref[peer, wave] for peer in range(stage_ref.shape[0])]
    rows = [
        jnp.concatenate([tile[:, start : start + times] for tile in tiles], axis=1)
        for start in range(0, LANES, times)
    ]
    return jnp.concatenate(rows, axis=0)


def transfer_kernel(group, members, times, me_ref, *refs):
    count = 1 + max(member[1] for member in members)
    arrays, refs = refs[:count], refs[count:]
    own_ref, own_extra_ref, *bessel_refs, out_ref, basis_ref, stage_ref = refs
    me = me_ref[0]
    step = pl.program_id(0)
    waves = out_ref.shape[0]
    extras = basis_ref.shape[1] // stage_ref.shape[3]

    def tiles(array, lead, rows):
        return arrays[array][rows] if lead is None else arrays[array][lead, rows]

    @pl.when(step == 0)
    def _():
        for apart, array, lead, _, at in members:
            extra = tiles(array, lead, pl.ds(at, extras)) if apart else own_extra_ref[...]
            basis_ref[apart] = extra.reshape(basis_ref.shape[1:])

    for number, (apart, array, lead, at, _) in enumerate(members):
        place = (number % group) ^ (me % group)
        rows = pl.ds(at + step * waves, waves)
        stage_ref[number // group, place] = tiles(array, lead, rows) if apart else own_ref[...]
    for wave in range(waves):
        total = None
        for number, bessel_ref in enumerate(bessel_refs):
            part = jnp.dot(
                source_rows(stage_ref.at[number], wave, times),
                bessel_ref[wave],
                preferred_element_type=jnp.float32,
            )
            total = part if total is None else total + part
        out_ref[wave] = total


def add_groups(me, group, arrays, members, own, bessel, times, extras):
    low_count = arrays[0].shape[-2]
    waves, _, multipoles = bessel.shape
    span = group * times
    cosmos = low_count * (LANES // times)
    block = math.gcd(waves, 8)
    in_specs = [pl.BlockSpec(memory_space=pltpu.VMEM)] * len(arrays)
    in_specs += [
        pl.BlockSpec((block, low_count, LANES), lambda s, me: (s, 0, 0)),
        pl.BlockSpec((extras, low_count, LANES), lambda s, me: (waves // extras, 0, 0)),
    ]
    in_specs += [
        pl.BlockSpec(
            (block, span, multipoles), lambda s, me, top=top: (s, (me[0] // group) ^ top, 0)
        )
        for top in TOPS[:-1]
    ]
    basis = (len(members) + group, extras * low_count, LANES)
    return pl.pallas_call(
        functools.partial(transfer_kernel, group, members, times),
        grid_spec=pltpu.PrefetchScalarGridSpec(
            num_scalar_prefetch=1,
            grid=(waves // block,),
            in_specs=in_specs,
            out_specs=[
                pl.BlockSpec((block, cosmos, multipoles), lambda s, me: (s, 0, 0)),
                pl.BlockSpec(basis, lambda s, me: (0, 0, 0)),
            ],
            scratch_shapes=[
                pltpu.VMEM((len(TOPS) - 1, group, block, low_count, LANES), jnp.bfloat16),
            ],
        ),
        out_shape=[
            jax.ShapeDtypeStruct((waves, cosmos, multipoles), jnp.float32),
            jax.ShapeDtypeStruct(basis, jnp.bfloat16),
        ],
        compiler_params=pltpu.CompilerParams(vmem_limit_bytes=24 << 20),
        cost_estimate=pl.CostEstimate(
            flops=16 * math.prod(bessel.shape) * cosmos,
            bytes_accessed=2 * math.prod(bessel.shape),
            transcendentals=0,
        ),
        name="transfer",
    )(me, *arrays, own, own, *[bessel] * (len(TOPS) - 1))


def power_kernel(times, chips, total_waves, *refs):
    piece_refs, traded_ref, extra_ref, held_ref, *refs = refs[: len(chips)], *refs[len(chips) :]
    rest_ref, params_ref, low_ref, high_ref, basis_ref, base_ref, out_ref, stage_ref, all_ref = refs
    waves, cosmos, multipoles = rest_ref.shape
    comps = base_ref.shape[1]
    peers = all_ref.shape[0]
    owned = multipoles // peers
    group = 2 * len(chips)
    me = lax.axis_index("ka")
    all_ref[...] = basis_ref[...]
    for low, (chip, piece_ref) in enumerate(zip(chips, piece_refs)):
        joined = low == len(chips) - 1
        for core in range(2):
            if core and not joined:
                piece = traded_ref[low]
            else:
                piece = piece_ref[core * waves : (core + 1) * waves]
            stage_ref[(2 * low + core) ^ (me % group)] = piece
            all_ref[2 * chip + core] = extra_ref[2 * low + core].reshape(all_ref.shape[1:])
    first_param, second_param = column(params_ref[0:1]), column(params_ref[1:2])
    low, high = column(low_ref[...]), column(high_ref[...])
    total = jnp.zeros((cosmos, multipoles), jnp.float32)
    for wave in range(waves):
        transfer = rest_ref[wave] + jnp.dot(
            source_rows(stage_ref, wave, times),
            held_ref[wave],
            preferred_element_type=jnp.float32,
        )
        index = (me * waves + wave).astype(jnp.float32)
        log_ratio = math.log(0.002) + index * (math.log(5000.0) / total_waves)
        tilted = 0.5 * first_param + 0.3 * second_param * log_ratio
        inside = (index >= low) & (index < high)
        factor = jnp.where(inside, jnp.exp(tilted), jnp.zeros_like(tilted)) / total_waves
        total = total + transfer * transfer * factor

    basis = jnp.concatenate([all_ref[peer ^ me][:owned] for peer in range(peers)], axis=0)
    power_high, power_low = split_two(total)
    basis_high, basis_low = basis[:, :comps], basis[:, comps:]
    part = base_ref[...]
    for left, right in (
        (power_low, basis_high),
        (power_high, basis_low),
        (power_high, basis_high),
    ):
        part = part - jnp.dot(left, right, preferred_element_type=jnp.float32)
    for peer in range(peers):
        own = total[:, peer * owned : (peer + 1) * owned]
        out_ref[peer] = fold(jnp.concatenate([own, part], axis=1))


def power_parts(pieces, traded, extras, held, rest, times, chips, total_waves, extra):
    low_count = traded.shape[2]
    waves, cosmos, multipoles = rest.shape
    basis, base = extra[-2:]
    peers = basis.shape[0]
    operands = [*pieces, traded, extras, held, rest, *extra]
    rows = folded_rows(cosmos, multipoles // peers + base.shape[1])
    return pl.pallas_call(
        functools.partial(power_kernel, times, chips, total_waves),
        in_specs=[pl.BlockSpec(memory_space=pltpu.VMEM)] * len(operands),
        out_specs=pl.BlockSpec(memory_space=pltpu.VMEM),
        out_shape=jax.ShapeDtypeStruct((peers, rows, LANES), jnp.float32),
        scratch_shapes=[
            pltpu.VMEM((2 * len(chips), waves, low_count, LANES), jnp.bfloat16),
            pltpu.VMEM(basis.shape, jnp.bfloat16),
        ],
        compiler_params=pltpu.CompilerParams(vmem_limit_bytes=24 << 20),
        cost_estimate=pl.CostEstimate(
            flops=16 * waves * held.shape[1] * multipoles * cosmos,
            bytes_accessed=2 * waves * held.shape[1] * multipoles,
            transcendentals=0,
        ),
        name="power",
    )(*operands)


def folds(rows, width):
    spare = LANES - width
    strips = width // spare if spare and width % spare == 0 else 0
    return strips if rows % (8 * (strips + 1)) == 0 else 0


def fold(value):
    rows, width = value.shape
    strips = folds(rows, width)
    if not strips:
        return jnp.concatenate([value, jnp.zeros((rows, LANES - width), value.dtype)], axis=1)
    spare = LANES - width
    head = rows * strips // (strips + 1)
    tail = [value[head:, strip * spare : (strip + 1) * spare] for strip in range(strips)]
    return jnp.concatenate([value[:head], jnp.concatenate(tail, axis=0)], axis=1)


def unfold(value, rows, width):
    strips = folds(rows, width)
    if not strips:
        return value[:, :width]
    size = rows // (strips + 1)
    tail = [value[strip * size : (strip + 1) * size, width:] for strip in range(strips)]
    return jnp.concatenate([value[:, :width], jnp.concatenate(tail, axis=1)], axis=0)


def folded_rows(rows, width):
    strips = folds(rows, width)
    return rows * strips // (strips + 1) if strips else rows


def near_mat(left, right, dims=((1,), (0,))):
    left_high, left_low = split_two(left)
    right_high, right_low = split_two(right)
    parts = ((left_low, right_high), (left_high, right_low), (left_high, right_high))
    return sum(
        lax.dot_general(one, other, (dims, ((), ())), preferred_element_type=jnp.float32)
        for one, other in parts
    )


def gradients_kernel(
    parts_ref,
    params_ref,
    coeffs_ref,
    inner_act_ref,
    inner_slope_ref,
    middle_act_ref,
    middle_slope_ref,
    weight_mid_ref,
    weight_out_ref,
    basis_ref,
    offset_ref,
    multipoles_ref,
    *refs,
):
    out_refs, (*value_refs, sems) = refs[:5], refs[5:]
    cosmos = params_ref.shape[1]
    owned, comps = basis_ref.shape
    copies = []

    def store(number, value):
        value_refs[number][...] = value
        copy = pltpu.make_async_copy(value_refs[number], out_refs[number], sems.at[number])
        copy.start()
        copies.append(copy)

    rows = ((0,), (0,))
    summed = unfold(jnp.sum(parts_ref[...], axis=0), cosmos, owned + comps)
    coef_grad = summed[:, owned : owned + comps] / cosmos
    middle_delta = near_mat(coef_grad, weight_out_ref[...]) * middle_slope_ref[...]
    store(3, near_mat(middle_delta, inner_act_ref[...], rows))
    inner_delta = near_mat(middle_delta, weight_mid_ref[...]) * inner_slope_ref[...]
    store(4, near_mat(coef_grad, middle_act_ref[...], rows))
    spectra = summed[:, :owned] * smoothing_of(multipoles_ref[...])
    coeffs = coeffs_ref[...]
    residual = offset_ref[...] + near_mat(coeffs, basis_ref[...], ((1,), (1,))) - spectra
    store(0, spectra.T)
    store(1, near_mat(residual, coeffs, rows) / cosmos)
    store(2, near_mat(params_ref[...], inner_delta))
    for copy in copies:
        copy.wait()


def gradients(parts, params, coeffs, hidden, weight_mid, weight_out, basis, offset, multipoles):
    count, cosmos = params.shape
    owned, comps = basis.shape
    width = weight_mid.shape[0]
    shapes = ((owned, cosmos), (owned, comps), (count, width), (width, width), (comps, width))
    operands = (parts, params, coeffs, *hidden, weight_mid, weight_out, basis)
    operands += (offset.reshape(1, owned), multipoles)
    return pl.pallas_call(
        gradients_kernel,
        in_specs=[pl.BlockSpec(memory_space=pltpu.VMEM)] * len(operands),
        out_specs=[pl.BlockSpec(memory_space=pl.ANY)] * len(shapes),
        out_shape=[jax.ShapeDtypeStruct(shape, jnp.float32) for shape in shapes],
        scratch_shapes=[pltpu.VMEM(shape, jnp.float32) for shape in shapes]
        + [pltpu.SemaphoreType.DMA((len(shapes),))],
        compiler_params=pltpu.CompilerParams(vmem_limit_bytes=24 << 20),
        name="gradients",
    )(*operands)


def exchange(value, apart, peers):
    return lax.ppermute(value, "ka", [(peer, peer ^ apart) for peer in range(peers)])


def after(value, *others):
    return lax.optimization_barrier((value, *others))[0]


def local(
    sources,
    bessel,
    multipoles,
    window_low,
    window_high,
    params,
    weight_in,
    bias_in,
    weight_mid,
    bias_mid,
    weight_out,
    bias_out,
    pca_basis,
    offset,
):
    waves = bessel.shape[0]
    total_waves = sources.shape[1]
    peers = total_waves // waves
    cosmos = params.shape[1]
    owned = multipoles.shape[0]
    group = LANES // waves
    half = group // 2
    times = sources.shape[0]
    extras = -(-owned // (cosmos * times // LANES))
    me = lax.axis_index("ka").astype(jnp.int32).reshape(1)
    own_multipoles = multipoles.reshape(1, owned)
    turned = jnp.transpose(sources, (0, 2, 1))

    chips = [top * half + low for top in TOPS for low in range(half)]
    late, last = chips[-half:], chips[-1]
    arranged = (turned, own_multipoles, pca_basis, bessel)
    ready = arrange(*arranged, TOPS[:FIRST], group, last)
    *rest_ready, give = arrange(*arranged, TOPS[FIRST:], group, last, HELD)
    held, rest_ready = dict(zip(HELD, rest_ready)), rest_ready[len(HELD) :]
    ready = dict(zip(chips, [*ready, *rest_ready]))
    got = {}
    near = [chip for chip in chips if 0 < chip < half]
    for chip in chips:
        if chip in (0, last):
            continue
        value = ready[chip]
        got[chip] = exchange(value, 2 * chip, peers)
    given = exchange(give, 1, peers)
    mine, other = ready[last], given[1]
    value = jnp.concatenate([mine, other[:waves]])
    got[last] = exchange(value, 2 * last, peers)

    others = lambda part, *then: jnp.stack([after(got[chip], *then)[waves:] for chip in part])
    early = [chip for chip in chips[:-half] if chip]
    traded = exchange(others(early), 1, peers)
    extra = [part for chip in chips[:half] for part in (got[chip][2 * waves :], traded[early.index(chip), waves:])]
    forwarded = exchange(jnp.stack(extra), TOPS[1] * group, peers)
    arrays = [traded, given] + [got[chip] for chip in early]
    members = []
    for chip in chips[:-half]:
        if chip:
            at = early.index(chip)
            members += [(2 * chip, 2 + at, None, 0, 2 * waves), (2 * chip + 1, 0, at, 0, waves)]
        else:
            members += [(0, 0, None, 0, waves), (1, 1, 0, 0, waves)]
    rest, basis = add_groups(me, group, arrays, members, ready[0], bessel, times, extras)
    late_traded = exchange(others(late[:-1], rest), 1, peers)

    inner_pre = mat(params.T, weight_in.T) + bias_in[None, :]
    inner_act = jax.nn.silu(inner_pre)
    middle_pre = mat(inner_act, weight_mid.T) + bias_mid[None, :]
    middle_act = jax.nn.silu(middle_pre)
    coeffs = mat(middle_act, weight_out.T) + bias_out[None, :]
    hidden = (inner_act, silu_slope(inner_pre), middle_act, silu_slope(middle_pre))
    base = mat(offset[None, :] + mat(coeffs, pca_basis.T), pca_basis)

    extra = (params, window_low.reshape(1, cosmos), window_high.reshape(1, cosmos), basis, base)
    pieces = [got[chip] for chip in late]
    parts = power_parts(pieces, late_traded, forwarded, held[TOPS[-1]], rest, times, late, total_waves, extra)
    gathered = lax.all_to_all(parts, "ka", split_axis=0, concat_axis=0, tiled=True)
    spectra, grad_basis, grad_in, grad_mid, grad_out = gradients(
        gathered, params, coeffs, hidden, weight_mid, weight_out, pca_basis, offset, own_multipoles
    )
    return (spectra, grad_basis, grad_in.T, grad_mid, grad_out)


def solution(mesh):
    return jax.shard_map(
        local,
        mesh=mesh,
        in_specs=(
            P("ka", None, "grp"),
            P("ka", None, None),
            P("ka"),
            P("grp"),
            P("grp"),
            P(None, "grp"),
            P(),
            P(),
            P(),
            P(),
            P(),
            P(),
            P("ka", None),
            P("ka"),
        ),
        out_specs=(
            P("ka", "grp"),
            P(("grp", "ka"), None),
            P("grp", None),
            P("grp", None),
            P("grp", None),
        ),
        check_vma=False,
    )
```

```python
import functools
import math

import jax
import jax.numpy as jnp
from jax import lax
from jax.experimental import pallas as pl
from jax.experimental.pallas import tpu as pltpu
from jax.sharding import PartitionSpec as P

LMAX = 5000
LANES = 128
TOPS = (2, 1, 0, 3)
HELD = (3,)
FIRST = 2
HIGHEST = lax.Precision.HIGHEST


def silu_slope(value):
    sigma = jax.nn.sigmoid(value)
    return sigma * (1.0 + value * (1.0 - sigma))


def mat(left, right, dims=((1,), (0,))):
    return lax.dot_general(
        left, right, (dims, ((), ())), precision=HIGHEST, preferred_element_type=jnp.float32
    )


def split_two(value):
    high = value.astype(jnp.bfloat16)
    low = (value - high.astype(jnp.float32)).astype(jnp.bfloat16)
    return high, low


def smoothing_of(multipoles):
    degree = multipoles.astype(jnp.float32)
    return jnp.exp(-2.0 * degree * (degree + 1.0) / (LMAX * (LMAX + 1.0)))


def column(row):
    return jnp.broadcast_to(row.astype(jnp.float32), (8, row.shape[1])).T[:, :1]


def smooth_basis(multipoles_ref, basis_ref, low_count):
    value = column(smoothing_of(multipoles_ref[...])) * basis_ref[...]
    value = jnp.concatenate([part.astype(jnp.float32) for part in split_two(value)], axis=1)
    spare = -value.shape[0] % low_count
    if spare:
        value = jnp.concatenate([value, jnp.zeros((spare, LANES), jnp.float32)], axis=0)
    return value.astype(jnp.bfloat16).reshape(-1, low_count, LANES)


def arrange_kernel(tops, group, last, waves, held_tops, source_ref, *refs):
    multipoles_ref, basis_ref, whole_ref, *refs = refs
    held_refs, refs = refs[: len(held_tops)], refs[len(held_tops) :]
    *out_refs, block_ref, rows_ref, turned_ref, sems, held_sems = refs
    _, times, cosmos, block = block_ref.shape
    packs = LANES // times
    low_count = cosmos // packs
    size = waves * low_count
    me = lax.axis_index("ka")
    copies = []
    for slot, top in enumerate(tops):
        start = pl.multiple_of(((me // group) ^ top) * block, block)
        copy = pltpu.make_async_copy(
            source_ref.at[:, :, pl.ds(start, block)], block_ref.at[slot], sems.at[slot]
        )
        copy.start()
        copies.append(copy)
    holds = []
    for slot, (top, held_ref) in enumerate(zip(held_tops, held_refs)):
        span = group * times
        start = pl.multiple_of(((me // group) ^ top) * span, span)
        copy = pltpu.make_async_copy(
            whole_ref.at[:, pl.ds(start, span), :], held_ref, held_sems.at[slot]
        )
        copy.start()
        holds.append(copy)
    extra = smooth_basis(multipoles_ref, basis_ref, low_count)
    chips = [top * group // 2 + low for top in tops for low in range(group // 2)]
    for slot, copy in enumerate(copies):
        copy.wait()
        rows = block_ref[slot].astype(jnp.float32).reshape(times * cosmos, block)
        rows_ref[: times * cosmos] = rows
        for low in range(low_count):
            pieces = [
                rows_ref[pl.ds(high * low_count + low, times, stride=cosmos), :]
                for high in range(packs)
            ]
            turned_ref[pl.ds(low, block, stride=low_count), :] = jnp.concatenate(pieces, axis=0).T
        for peer in range(group):
            start = pl.multiple_of((peer ^ (me % group)) * size, size)
            piece = turned_ref[pl.ds(start, size), :].astype(jnp.bfloat16)
            piece = piece.reshape(waves, low_count, LANES)
            chip, core = tops[slot] * group // 2 + peer // 2, peer % 2
            out_ref = out_refs[chips.index(chip)]
            if chip in (0, last):
                out_ref = out_refs[-1].at[int(chip == last)] if core else out_ref
                out_ref[:waves] = piece
                if core or chip == 0:
                    out_ref[waves:] = extra
            else:
                out_ref[core * waves : (core + 1) * waves] = piece
                if tops[slot] != TOPS[-1]:
                    out_ref[2 * waves :] = extra
    for copy in holds:
        copy.wait()


def arrange(sources, multipoles, basis, bessel, tops, group, last, held_tops=()):
    times, cosmos, total = sources.shape
    waves, _, multipole_count = bessel.shape
    low_count = cosmos // (LANES // times)
    block = waves * group
    extras = -(-basis.shape[0] // low_count)
    one, two = (count * waves + extras for count in (1, 2))
    chips = [top * group // 2 + low for top in tops for low in range(group // 2)]
    late = range(TOPS[-1] * group // 2, TOPS[-1] * group // 2 + group // 2)
    tiles = [(one if chip in (0, last) else two) - (extras if chip in late else 0) for chip in chips]
    shapes = [(count, low_count, LANES) for count in tiles]
    if last in chips:
        shapes.append((2, one, low_count, LANES))
    held = pltpu.VMEM((waves, group * times, multipole_count), bessel.dtype)
    vmem, anywhere = (pl.BlockSpec(memory_space=space) for space in (pltpu.VMEM, pl.ANY))
    return pl.pallas_call(
        functools.partial(arrange_kernel, tops, group, last, waves, held_tops),
        in_specs=[anywhere, vmem, vmem, anywhere],
        out_specs=[vmem] * (len(held_tops) + len(shapes)),
        out_shape=[held] * len(held_tops)
        + [jax.ShapeDtypeStruct(shape, jnp.bfloat16) for shape in shapes],
        scratch_shapes=[
            pltpu.VMEM((len(tops), times, cosmos, block), jnp.bfloat16),
            pltpu.VMEM(((times + 1) * cosmos, block), jnp.float32),
            pltpu.VMEM(((block + 1) * low_count, LANES), jnp.float32),
            pltpu.SemaphoreType.DMA((len(tops),)),
            pltpu.SemaphoreType.DMA((max(1, len(held_tops)),)),
        ],
        compiler_params=pltpu.CompilerParams(vmem_limit_bytes=(24 if held_tops else 61) << 20),
        cost_estimate=pl.CostEstimate(
            flops=0, bytes_accessed=16 * times * cosmos * block * len(tops), transcendentals=0
        ),
        name="arrange",
    )(sources, multipoles, basis, bessel)


def source_rows(stage_ref, wave, times):
    tiles = [stage_ref[peer, wave] for peer in range(stage_ref.shape[0])]
    rows = [
        jnp.concatenate([tile[:, start : start + times] for tile in tiles], axis=1)
        for start in range(0, LANES, times)
    ]
    return jnp.concatenate(rows, axis=0)


def transfer_kernel(group, members, times, me_ref, *refs):
    count = 1 + max(member[1] for member in members)
    arrays, refs = refs[:count], refs[count:]
    own_ref, own_extra_ref, *bessel_refs, out_ref, basis_ref, stage_ref = refs
    me = me_ref[0]
    step = pl.program_id(0)
    waves = out_ref.shape[0]
    extras = basis_ref.shape[1] // stage_ref.shape[3]

    def tiles(array, lead, rows):
        return arrays[array][rows] if lead is None else arrays[array][lead, rows]

    @pl.when(step == 0)
    def _():
        for apart, array, lead, _, at in members:
            extra = tiles(array, lead, pl.ds(at, extras)) if apart else own_extra_ref[...]
            basis_ref[apart] = extra.reshape(basis_ref.shape[1:])

    for number, (apart, array, lead, at, _) in enumerate(members):
        place = (number % group) ^ (me % group)
        rows = pl.ds(at + step * waves, waves)
        stage_ref[number // group, place] = tiles(array, lead, rows) if apart else own_ref[...]
    for wave in range(waves):
        total = None
        for number, bessel_ref in enumerate(bessel_refs):
            part = jnp.dot(
                source_rows(stage_ref.at[number], wave, times),
                bessel_ref[wave],
                preferred_element_type=jnp.float32,
            )
            total = part if total is None else total + part
        out_ref[wave] = total


def add_groups(me, group, arrays, members, own, bessel, times, extras):
    low_count = arrays[0].shape[-2]
    waves, _, multipoles = bessel.shape
    span = group * times
    cosmos = low_count * (LANES // times)
    block = math.gcd(waves, 8)
    in_specs = [pl.BlockSpec(memory_space=pltpu.VMEM)] * len(arrays)
    in_specs += [
        pl.BlockSpec((block, low_count, LANES), lambda s, me: (s, 0, 0)),
        pl.BlockSpec((extras, low_count, LANES), lambda s, me: (waves // extras, 0, 0)),
    ]
    in_specs += [
        pl.BlockSpec(
            (block, span, multipoles), lambda s, me, top=top: (s, (me[0] // group) ^ top, 0)
        )
        for top in TOPS[:-1]
    ]
    basis = (len(members) + group, extras * low_count, LANES)
    return pl.pallas_call(
        functools.partial(transfer_kernel, group, members, times),
        grid_spec=pltpu.PrefetchScalarGridSpec(
            num_scalar_prefetch=1,
            grid=(waves // block,),
            in_specs=in_specs,
            out_specs=[
                pl.BlockSpec((block, cosmos, multipoles), lambda s, me: (s, 0, 0)),
                pl.BlockSpec(basis, lambda s, me: (0, 0, 0)),
            ],
            scratch_shapes=[
                pltpu.VMEM((len(TOPS) - 1, group, block, low_count, LANES), jnp.bfloat16),
            ],
        ),
        out_shape=[
            jax.ShapeDtypeStruct((waves, cosmos, multipoles), jnp.float32),
            jax.ShapeDtypeStruct(basis, jnp.bfloat16),
        ],
        compiler_params=pltpu.CompilerParams(vmem_limit_bytes=24 << 20),
        cost_estimate=pl.CostEstimate(
            flops=16 * math.prod(bessel.shape) * cosmos,
            bytes_accessed=2 * math.prod(bessel.shape),
            transcendentals=0,
        ),
        name="transfer",
    )(me, *arrays, own, own, *[bessel] * (len(TOPS) - 1))


def power_kernel(times, chips, total_waves, *refs):
    piece_refs, traded_ref, extra_ref, held_ref, *refs = refs[: len(chips)], *refs[len(chips) :]
    rest_ref, params_ref, low_ref, high_ref, basis_ref, base_ref, out_ref, stage_ref, all_ref = refs
    waves, cosmos, multipoles = rest_ref.shape
    comps = base_ref.shape[1]
    peers = all_ref.shape[0]
    owned = multipoles // peers
    group = 2 * len(chips)
    me = lax.axis_index("ka")
    all_ref[...] = basis_ref[...]
    for low, (chip, piece_ref) in enumerate(zip(chips, piece_refs)):
        joined = low == len(chips) - 1
        for core in range(2):
            if core and not joined:
                piece = traded_ref[low]
            else:
                piece = piece_ref[core * waves : (core + 1) * waves]
            stage_ref[(2 * low + core) ^ (me % group)] = piece
            all_ref[2 * chip + core] = extra_ref[2 * low + core].reshape(all_ref.shape[1:])
    first_param, second_param = column(params_ref[0:1]), column(params_ref[1:2])
    low, high = column(low_ref[...]), column(high_ref[...])
    total = jnp.zeros((cosmos, multipoles), jnp.float32)
    for wave in range(waves):
        transfer = rest_ref[wave] + jnp.dot(
            source_rows(stage_ref, wave, times),
            held_ref[wave],
            preferred_element_type=jnp.float32,
        )
        index = (me * waves + wave).astype(jnp.float32)
        log_ratio = math.log(0.002) + index * (math.log(5000.0) / total_waves)
        tilted = 0.5 * first_param + 0.3 * second_param * log_ratio
        inside = (index >= low) & (index < high)
        factor = jnp.where(inside, jnp.exp(tilted), jnp.zeros_like(tilted)) / total_waves
        total = total + transfer * transfer * factor

    basis = jnp.concatenate([all_ref[peer ^ me][:owned] for peer in range(peers)], axis=0)
    power_high, power_low = split_two(total)
    basis_high, basis_low = basis[:, :comps], basis[:, comps:]
    part = base_ref[...]
    for left, right in (
        (power_low, basis_high),
        (power_high, basis_low),
        (power_high, basis_high),
    ):
        part = part - jnp.dot(left, right, preferred_element_type=jnp.float32)
    for peer in range(peers):
        own = total[:, peer * owned : (peer + 1) * owned]
        out_ref[peer] = fold(jnp.concatenate([own, part], axis=1))


def power_parts(pieces, traded, extras, held, rest, times, chips, total_waves, extra):
    low_count = traded.shape[2]
    waves, cosmos, multipoles = rest.shape
    basis, base = extra[-2:]
    peers = basis.shape[0]
    operands = [*pieces, traded, extras, held, rest, *extra]
    rows = folded_rows(cosmos, multipoles // peers + base.shape[1])
    return pl.pallas_call(
        functools.partial(power_kernel, times, chips, total_waves),
        in_specs=[pl.BlockSpec(memory_space=pltpu.VMEM)] * len(operands),
        out_specs=pl.BlockSpec(memory_space=pltpu.VMEM),
        out_shape=jax.ShapeDtypeStruct((peers, rows, LANES), jnp.float32),
        scratch_shapes=[
            pltpu.VMEM((2 * len(chips), waves, low_count, LANES), jnp.bfloat16),
            pltpu.VMEM(basis.shape, jnp.bfloat16),
        ],
        compiler_params=pltpu.CompilerParams(vmem_limit_bytes=24 << 20),
        cost_estimate=pl.CostEstimate(
            flops=16 * waves * held.shape[1] * multipoles * cosmos,
            bytes_accessed=2 * waves * held.shape[1] * multipoles,
            transcendentals=0,
        ),
        name="power",
    )(*operands)


def folds(rows, width):
    spare = LANES - width
    strips = width // spare if spare and width % spare == 0 else 0
    return strips if rows % (8 * (strips + 1)) == 0 else 0


def fold(value):
    rows, width = value.shape
    strips = folds(rows, width)
    if not strips:
        return jnp.concatenate([value, jnp.zeros((rows, LANES - width), value.dtype)], axis=1)
    spare = LANES - width
    head = rows * strips // (strips + 1)
    tail = [value[head:, strip * spare : (strip + 1) * spare] for strip in range(strips)]
    return jnp.concatenate([value[:head], jnp.concatenate(tail, axis=0)], axis=1)


def unfold(value, rows, width):
    strips = folds(rows, width)
    if not strips:
        return value[:, :width]
    size = rows // (strips + 1)
    tail = [value[strip * size : (strip + 1) * size, width:] for strip in range(strips)]
    return jnp.concatenate([value[:, :width], jnp.concatenate(tail, axis=1)], axis=0)


def folded_rows(rows, width):
    strips = folds(rows, width)
    return rows * strips // (strips + 1) if strips else rows


def near_mat(left, right, dims=((1,), (0,))):
    left_high, left_low = split_two(left)
    right_high, right_low = split_two(right)
    parts = ((left_low, right_high), (left_high, right_low), (left_high, right_high))
    return sum(
        lax.dot_general(one, other, (dims, ((), ())), preferred_element_type=jnp.float32)
        for one, other in parts
    )


def gradients_kernel(
    parts_ref,
    params_ref,
    coeffs_ref,
    inner_act_ref,
    inner_slope_ref,
    middle_act_ref,
    middle_slope_ref,
    weight_mid_ref,
    weight_out_ref,
    basis_ref,
    offset_ref,
    multipoles_ref,
    *refs,
):
    out_refs, (*value_refs, sems) = refs[:5], refs[5:]
    cosmos = params_ref.shape[1]
    owned, comps = basis_ref.shape
    copies = []

    def store(number, value):
        value_refs[number][...] = value
        copy = pltpu.make_async_copy(value_refs[number], out_refs[number], sems.at[number])
        copy.start()
        copies.append(copy)

    rows = ((0,), (0,))
    summed = unfold(jnp.sum(parts_ref[...], axis=0), cosmos, owned + comps)
    coef_grad = summed[:, owned : owned + comps] / cosmos
    middle_delta = near_mat(coef_grad, weight_out_ref[...]) * middle_slope_ref[...]
    store(3, near_mat(middle_delta, inner_act_ref[...], rows))
    inner_delta = near_mat(middle_delta, weight_mid_ref[...]) * inner_slope_ref[...]
    store(4, near_mat(coef_grad, middle_act_ref[...], rows))
    spectra = summed[:, :owned] * smoothing_of(multipoles_ref[...])
    coeffs = coeffs_ref[...]
    residual = offset_ref[...] + near_mat(coeffs, basis_ref[...], ((1,), (1,))) - spectra
    store(0, spectra.T)
    store(1, near_mat(residual, coeffs, rows) / cosmos)
    store(2, near_mat(params_ref[...], inner_delta))
    for copy in copies:
        copy.wait()


def gradients(parts, params, coeffs, hidden, weight_mid, weight_out, basis, offset, multipoles):
    count, cosmos = params.shape
    owned, comps = basis.shape
    width = weight_mid.shape[0]
    shapes = ((owned, cosmos), (owned, comps), (count, width), (width, width), (comps, width))
    operands = (parts, params, coeffs, *hidden, weight_mid, weight_out, basis)
    operands += (offset.reshape(1, owned), multipoles)
    return pl.pallas_call(
        gradients_kernel,
        in_specs=[pl.BlockSpec(memory_space=pltpu.VMEM)] * len(operands),
        out_specs=[pl.BlockSpec(memory_space=pl.ANY)] * len(shapes),
        out_shape=[jax.ShapeDtypeStruct(shape, jnp.float32) for shape in shapes],
        scratch_shapes=[pltpu.VMEM(shape, jnp.float32) for shape in shapes]
        + [pltpu.SemaphoreType.DMA((len(shapes),))],
        compiler_params=pltpu.CompilerParams(vmem_limit_bytes=24 << 20),
        name="gradients",
    )(*operands)


def exchange(value, apart, peers):
    return lax.ppermute(value, "ka", [(peer, peer ^ apart) for peer in range(peers)])


def after(value, *others):
    return lax.optimization_barrier((value, *others))[0]


def local(
    sources,
    bessel,
    multipoles,
    window_low,
    window_high,
    params,
    weight_in,
    bias_in,
    weight_mid,
    bias_mid,
    weight_out,
    bias_out,
    pca_basis,
    offset,
):
    waves = bessel.shape[0]
    total_waves = sources.shape[1]
    peers = total_waves // waves
    cosmos = params.shape[1]
    owned = multipoles.shape[0]
    group = LANES // waves
    half = group // 2
    times = sources.shape[0]
    extras = -(-owned // (cosmos * times // LANES))
    me = lax.axis_index("ka").astype(jnp.int32).reshape(1)
    own_multipoles = multipoles.reshape(1, owned)
    turned = jnp.transpose(sources, (0, 2, 1))

    chips = [top * half + low for top in TOPS for low in range(half)]
    late, last = chips[-half:], chips[-1]
    arranged = (turned, own_multipoles, pca_basis, bessel)
    ready = arrange(*arranged, TOPS[:FIRST], group, last)
    *rest_ready, give = arrange(*arranged, TOPS[FIRST:], group, last, HELD)
    held, rest_ready = dict(zip(HELD, rest_ready)), rest_ready[len(HELD) :]
    ready = dict(zip(chips, [*ready, *rest_ready]))
    got = {}
    near = [chip for chip in chips if 0 < chip < half]
    for chip in chips:
        if chip in (0, last):
            continue
        value = ready[chip]
        got[chip] = exchange(value, 2 * chip, peers)
    given = exchange(give, 1, peers)
    mine, other = ready[last], given[1]
    value = jnp.concatenate([mine, other[:waves]])
    got[last] = exchange(value, 2 * last, peers)

    others = lambda part, *then: jnp.stack([after(got[chip], *then)[waves:] for chip in part])
    early = [chip for chip in chips[:-half] if chip]
    traded = exchange(others(early), 1, peers)
    extra = [part for chip in chips[:half] for part in (got[chip][2 * waves :], traded[early.index(chip), waves:])]
    forwarded = exchange(jnp.stack(extra), TOPS[1] * group, peers)
    arrays = [traded, given] + [got[chip] for chip in early]
    members = []
    for chip in chips[:-half]:
        if chip:
            at = early.index(chip)
            members += [(2 * chip, 2 + at, None, 0, 2 * waves), (2 * chip + 1, 0, at, 0, waves)]
        else:
            members += [(0, 0, None, 0, waves), (1, 1, 0, 0, waves)]
    rest, basis = add_groups(me, group, arrays, members, ready[0], bessel, times, extras)
    late_traded = exchange(others(late[:-1], rest), 1, peers)

    inner_pre = mat(params.T, weight_in.T) + bias_in[None, :]
    inner_act = jax.nn.silu(inner_pre)
    middle_pre = mat(inner_act, weight_mid.T) + bias_mid[None, :]
    middle_act = jax.nn.silu(middle_pre)
    coeffs = mat(middle_act, weight_out.T) + bias_out[None, :]
    hidden = (inner_act, silu_slope(inner_pre), middle_act, silu_slope(middle_pre))
    base = mat(offset[None, :] + mat(coeffs, pca_basis.T), pca_basis)

    extra = (params, window_low.reshape(1, cosmos), window_high.reshape(1, cosmos), basis, base)
    pieces = [got[chip] for chip in late]
    parts = power_parts(pieces, late_traded, forwarded, held[TOPS[-1]], rest, times, late, total_waves, extra)
    gathered = lax.all_to_all(parts, "ka", split_axis=0, concat_axis=0, tiled=True)
    spectra, grad_basis, grad_in, grad_mid, grad_out = gradients(
        gathered, params, coeffs, hidden, weight_mid, weight_out, pca_basis, offset, own_multipoles
    )
    return (spectra, grad_basis, grad_in.T, grad_mid, grad_out)


def solution(mesh):
    return jax.shard_map(
        local,
        mesh=mesh,
        in_specs=(
            P("ka", None, "grp"),
            P("ka", None, None),
            P("ka"),
            P("grp"),
            P("grp"),
            P(None, "grp"),
            P(),
            P(),
            P(),
            P(),
            P(),
            P(),
            P("ka", None),
            P("ka"),
        ),
        out_specs=(
            P("ka", "grp"),
            P(("grp", "ka"), None),
            P("grp", None),
            P("grp", None),
            P("grp", None),
        ),
        check_vma=False,
    )
```
